256 devices in a mesh: sec: 4 (over z_hi), gx: 16 (over x, y), gy: 4 (over z_lo, core).
Axes of the slice: x: 4, y: 4, z: 8 (z_hi: 4, z_lo: 2; z = z_hi * 2 + z_lo), core: 2. Of those that a mesh axis runs over, the one named last changes fastest.
Arguments:
- reg_disp: float32 [1024, 256, 256], P(('sec', 'gx'), 'gy'), may hold values from -6 to 6
- reg_prev: float32 [1024, 256, 256], P(('sec', 'gx'), 'gy'), may hold values from -6 to 6
- reg_coef: float32 [1024, 256, 256], P(('sec', 'gx'), 'gy'), may hold values from 0.02 to 0.15
- basin_disp: float32 [4, 64, 32768], P('sec', None, ('gx', 'gy')), may hold values from -4 to 4
- face_index: int32 [4, 32768], P('sec', ('gx', 'gy')), may hold values from 0 to 65535, as said below
- soil_class: int32 [4, 64, 32768], P('sec', None, ('gx', 'gy')), may hold values from 0 to 7, as said below
- spring_count: int32 [8], replicated, may hold values from 1 to 16, as said below
- spring_modulus: float32 [8, 16], replicated, may hold values from 0.02 to 0.1
- spring_yield: float32 [8, 16], replicated, may hold values from 0.005 to 0.05
Outputs:
- reg_final: float32 [1024, 256, 256], P(('sec', 'gx'), 'gy')
- basin_final: float32 [4, 64, 32768], P('sec', None, ('gx', 'gy'))
The draws below stay inside these ranges and needn't reach their ends.
Inputs may be any that keep to these rules, and one draw needn't show every extreme that they name: `face_index`: a cell of the quarter's face; in every quarter some column uses the first face cell and some column the last. `soil_class`: soil class ids. `spring_count`: some class has 16 springs and some class has one.
All inputs are finite; a program needn't handle non-finite values.
Results may differ from the reference program's by a relative error of at most 0.0002.
Values sent between devices are 32-bit elements; how exact they have to be, the bound alone decides.
No kernel may reach another device: no remote copies, remote signals or barrier semaphores. Data moves between devices by JAX's collectives and lax.ppermute only.
A program may use at most 128 MiB of HBM per device.

```python
import math
import jax
import jax.numpy as jnp
from jax import lax

CX = 16
CZ = 256
LZ = 64
COLS_DEV = 512
NSPR = 16
NCLASS = 8
STEPS = 8
NX = 1024
NY = 256
NQ = 4
COLS_Q = 32768
FDEP = 64
N_SEC = 4
N_GX = 16


def draw_face_index(key, part):
    key = jax.random.fold_in(key, 37)
    quarter_x = CX * N_GX
    flat = jax.random.randint(key, (NQ, COLS_Q), 0, quarter_x * NY)
    flat = flat.at[:, 0].set(0)
    flat = flat.at[:, COLS_Q - 1].set(quarter_x * NY - 1)
    return flat.astype(jnp.int32)


def draw_soil_class(key, part):
    key = jax.random.fold_in(key, 11)
    first, second = jax.random.split(key)
    regions = jax.random.randint(first, (NQ, 1, COLS_Q // COLS_DEV), 0, NCLASS)
    spread = jnp.repeat(regions, COLS_DEV, axis=2)
    jitter = jax.random.randint(second, (NQ, LZ, COLS_Q), 0, 3)
    return ((spread + jitter) % NCLASS).astype(jnp.int32)


def draw_spring_count(key, part):
    key = jax.random.fold_in(key, 23)
    first, second = jax.random.split(key)
    counts = jax.random.randint(first, (NCLASS,), 1, NSPR + 1)
    chosen = jax.random.randint(second, (), 0, NCLASS)
    counts = counts.at[chosen].set(NSPR)
    counts = counts.at[(chosen + 1) % NCLASS].set(1)
    return counts.astype(jnp.int32)


def level_of(own_key, extent, pieces, least, top_value):
    level, own = 1.0, jax.random.fold_in(own_key, 6)
    for dim, blocks in pieces:
        draws = jnp.exp(jax.random.uniform(jax.random.fold_in(own, dim), (blocks,), jnp.float32, least / len(pieces), top_value / len(pieces)))
        level = level * jnp.repeat(draws, extent[dim] // blocks).reshape([-1 if axis == dim else 1 for axis in range(len(extent))])
    return level


def noise(key, dims, scale, most, cuts=(), kind=jnp.bfloat16):
    result = scale * jax.random.normal(key, dims, jnp.float32)
    if cuts:
        result = result * level_of(key, dims, cuts, -0.22, 0.18)
    return jnp.clip(result, -most, most).astype(kind)


def setup_inputs(seed: int = 0) -> dict:
    streams_of = jax.random.split(jax.random.key(seed), 10)
    reg_disp = noise(streams_of[0], (NX, NY, CZ), 1.0, 6.0, ((0, 64), (1, 4)), jnp.float32)
    reg_prev = noise(streams_of[1], (NX, NY, CZ), 1.0, 6.0, ((0, 64), (1, 4)), jnp.float32)
    reg_coef = jnp.clip(jnp.exp(math.log(0.15) - 2.014903 * jax.random.uniform(streams_of[2], (NX, NY, CZ), jnp.float32) ** level_of(streams_of[2], (NX, NY, CZ), ((0, 64), (1, 4)), -0.2, 0.2)), 0.02, 0.15)
    basin_disp = noise(streams_of[3], (NQ, LZ, COLS_Q), 0.5, 4.0, ((0, 4), (2, 64)), jnp.float32)
    face_index = draw_face_index(jax.random.fold_in(streams_of[9], 71), 0)
    soil_class = draw_soil_class(jax.random.fold_in(streams_of[9], 71), 0)
    spring_count = draw_spring_count(jax.random.fold_in(streams_of[9], 71), 0)
    spring_modulus = jnp.clip(jnp.exp(jax.random.uniform(streams_of[7], (NCLASS, NSPR), jnp.float32, math.log(0.02), math.log(0.1))), 0.02, 0.1)
    spring_yield = jnp.clip(jnp.exp(jax.random.uniform(streams_of[8], (NCLASS, NSPR), jnp.float32, math.log(0.005), math.log(0.05))), 0.005, 0.05)
    return {"reg_disp": reg_disp, "reg_prev": reg_prev, "reg_coef": reg_coef, "basin_disp": basin_disp, "face_index": face_index, "soil_class": soil_class, "spring_count": spring_count, "spring_modulus": spring_modulus, "spring_yield": spring_yield}


stress_rate = 0.5


def laplace_rim(padded, center):
    above = jnp.concatenate([center[:, :, :1], center[:, :, :-1]], axis=2)
    below = jnp.concatenate([center[:, :, 1:], jnp.zeros_like(center[:, :, :1])], axis=2)
    beside = padded[2:, 1:-1] + padded[:-2, 1:-1] + padded[1:-1, 2:] + padded[1:-1, :-2]
    return beside + above + below - 6.0 * center


def spring_tables(soil, spring_count, spring_modulus, spring_yield):
    classes = jnp.arange(spring_count.shape[0], dtype=jnp.int32)
    matches = soil[None] == classes[:, None, None]
    onehot = matches.astype(spring_modulus.dtype)
    modulus = jnp.einsum('ck,clx->klx', spring_modulus, onehot, precision=lax.Precision.HIGHEST)
    limits = jnp.einsum('ck,clx->klx', spring_yield, onehot, precision=lax.Precision.HIGHEST)
    count_cell = jnp.sum(jnp.where(matches, spring_count[:, None, None], 0), axis=0).astype(jnp.int32)
    levels = jnp.arange(spring_modulus.shape[1], dtype=jnp.int32)
    active = (levels[:, None, None] < count_cell[None]).astype(spring_modulus.dtype)
    return modulus, limits * active


def column_motion(displace, velocity, stress):
    above = jnp.concatenate([jnp.zeros_like(stress[:1]), stress[:-1]], axis=0)
    velocity = velocity + stress_rate * (stress - above)
    return displace + velocity, velocity


def reference(reg_disp, reg_prev, reg_coef, basin_disp, face_index, soil_class, spring_count, spring_modulus, spring_yield):
    current, former = reg_disp, reg_prev
    planes = []
    for step in range(STEPS):
        padded = jnp.pad(current, ((1, 1), (1, 1), (0, 0)))
        following = 2.0 * current - former + reg_coef * laplace_rim(padded, current)
        former, current = current, following
        planes.append(current[:, :, FDEP])
    trace = jnp.stack(planes)
    quarter_x = CX * N_GX
    results = []
    for quarter in range(N_SEC):
        face = trace[:, quarter * quarter_x:(quarter + 1) * quarter_x, :].reshape(STEPS, quarter_x * NY)
        base = jnp.take(face, face_index[quarter], axis=1)
        modulus, limits = spring_tables(soil_class[quarter], spring_count, spring_modulus, spring_yield)
        displace = basin_disp[quarter]
        velocity = jnp.zeros_like(displace)
        springs = jnp.zeros_like(modulus)
        strain_old = jnp.zeros_like(displace)
        for step in range(STEPS):
            lower = jnp.concatenate([displace[1:], base[step][None]], axis=0)
            strain = lower - displace
            springs = jnp.clip(springs + modulus * (strain - strain_old)[None], -limits, limits)
            stress = jnp.sum(springs, axis=0)
            strain_old = strain
            displace, velocity = column_motion(displace, velocity, stress)
        results.append(displace)
    return current, jnp.stack(results)
```

```python
import functools
import jax
import jax.numpy as jnp
from jax import lax
from jax.experimental import pallas as pl
from jax.experimental.pallas import tpu as pltpu
from jax.sharding import PartitionSpec as P

STEPS = 8
HALO = 8
FDEP = 64
stress_rate = 0.5
XAX = ("sec", "gx")
F32 = jnp.float32
ANY = pl.BlockSpec(memory_space=pl.ANY)
VM = pl.BlockSpec(memory_space=pltpu.VMEM)
SM = pl.BlockSpec(memory_space=pltpu.SMEM)
PARAMS = pltpu.CompilerParams(vmem_limit_bytes=48 * 1024 * 1024)


def sds(*shape):
    return jax.ShapeDtypeStruct(shape, F32)


def x_edges():
    at = lax.axis_index("sec") * lax.axis_size("gx") + lax.axis_index("gx")
    return at == 0, at == lax.axis_size("sec") * lax.axis_size("gx") - 1


def y_edges():
    at = lax.axis_index("gy")
    return at == 0, at == lax.axis_size("gy") - 1


def lanes(shape):
    return lax.broadcasted_iota(jnp.int32, shape, len(shape) - 1)


def band_kernel(u, p, c, band, to_right, to_left):
    lane = lanes((64, 128))
    for x in range(8):
        halves = []
        for row in (x, x + 8):
            halves.append(
                jnp.where(
                    lane < 73,
                    u[row],
                    jnp.where(lane < 88, pltpu.roll(p[row], 16, 1), pltpu.roll(c[row], 31, 1)),
                )
            )
        turned = jnp.concatenate(halves, axis=0).T
        band[:, x, :] = turned[56:104]
    first = lanes((8, 128)) < 64
    for k in range(24):
        a, b = band[k], band[k + 24]
        ra, rb = pltpu.roll(a, 64, 1), pltpu.roll(b, 64, 1)
        to_right[k] = jnp.where(first, ra, b)
        to_left[k] = jnp.where(first, a, rb)


def band_edges_kernel(band, from_left, from_right, ext, send_a, send_b):
    low_edge, high_edge = x_edges()
    even = lax.rem(lax.axis_index("gy"), 2) == 0
    lane = lanes((8, 128))
    first = lane < 64
    group = lanes((32, 128)) // 8
    for g in range(3):
        high = jnp.zeros((32, 128), F32)
        low = jnp.zeros((32, 128), F32)
        for q in range(16):
            level = g * 16 + q
            own = band[level]
            near = from_right[level % 24]
            far = from_left[level % 24]
            if level >= 24:
                near, far = pltpu.roll(near, 64, 1), pltpu.roll(far, 64, 1)
            near = jnp.where(high_edge, 0.0, near)
            far = jnp.where(low_edge, 0.0, far)
            full = jnp.concatenate([own, pltpu.roll(own, 64, 1), near, far], axis=0)
            ext[level] = full
            high = jnp.where(group == q, pltpu.roll(full, (q * 8 - 56) % 128, 1), high)
            low = jnp.where(group == q, pltpu.roll(full, q * 8, 1), low)
        send_a[g] = jnp.where(even, high, low)
        send_b[g] = jnp.where(even, low, high)


def band_steps_kernel(ext, recv_a, recv_b, trace, one, two, coef):
    low_edge, high_edge = y_edges()
    even = lax.rem(lax.axis_index("gy"), 2) == 0
    lane = lanes((32, 128))
    for g in range(3):
        a, b = recv_a[g], recv_b[g]
        high = jnp.where(high_edge, 0.0, jnp.where(even, a, b))
        low = jnp.where(low_edge, 0.0, jnp.where(even, b, a))
        for q in range(16):
            level = g * 16 + q
            if level > 46:
                continue
            full = jnp.where(
                lane < 64,
                ext[level],
                jnp.where(
                    lane < 72,
                    pltpu.roll(high, (64 - q * 8) % 128, 1),
                    jnp.where(lane >= 120, pltpu.roll(low, (120 - q * 8) % 128, 1), 0.0),
                ),
            )
            if level < 17:
                one[level] = full
            elif level < 32:
                two[level - 16] = full
            else:
                coef[level - 31] = full
    first = lanes((8, 128)) < 64
    now, old = one, two
    for step in range(1, STEPS + 1):
        for j in range(step, 17 - step):
            u = now[j]
            beside = pltpu.roll(u, 1, 0) + pltpu.roll(u, 31, 0) + pltpu.roll(u, 1, 1) + pltpu.roll(u, 127, 1)
            lap = beside + now[j - 1] + now[j + 1] - 6.0 * u
            old[j] = 2.0 * u - old[j] + coef[j] * lap
        now, old = old, now
        plane = now[8]
        trace[:, step - 1, :] = jnp.where(first, plane[0:8], pltpu.roll(plane[8:16], 64, 1))


def pick_kernel(table, index, out):
    me = lax.axis_index("gx")

    def tile(t, carry):
        cell = jnp.broadcast_to(index[pl.ds(t, 1), :], (8, 128))
        x, y = cell >> 8, cell & 255
        place = ((y >> 6) << 3) + (x & 7)
        place = jnp.where((x >> 4) == me, place, -1)
        lane = (((x >> 3) & 1) << 6) + (y & 63)
        acc = jnp.zeros((8, 128), F32)
        for k in range(32):
            acc = jnp.where(place == k, jnp.take_along_axis(table[k], lane, axis=1), acc)
        out[t] = acc
        return carry

    lax.fori_loop(0, index.shape[0], tile, 0)


def spring_values(cls, k, count, modulus, yields):
    mod = jnp.zeros(cls.shape, F32)
    lim = jnp.zeros(cls.shape, F32)
    for c in range(8):
        hit = cls == c
        mod = jnp.where(hit, modulus[c, k], mod)
        lim = jnp.where(hit, jnp.where(k < count[c], yields[c, k], 0.0), lim)
    return mod, lim


def columns_kernel(count, modulus, yields, soil, start, out, edge, mods, lims, springs):
    def rows(r, carry):
        at = pl.ds(pl.multiple_of(r * 8, 8), 8)
        cls = soil[at, :]
        for k in range(16):
            mod, lim = spring_values(cls, k, count, modulus, yields)
            mods[k, at, :] = mod
            lims[k, at, :] = lim
            springs[k, at, :] = jnp.zeros((8, 128), F32)
        return carry

    lax.fori_loop(0, 8, rows, 0)
    row = lax.broadcasted_iota(jnp.int32, (64, 128), 0)

    def step(s, state):
        disp, vel, old = state
        strain = pltpu.roll(disp, 63, 0) - disp
        inc = strain - old
        stress = jnp.zeros((64, 128), F32)
        for k in range(16):
            lim = lims[k]
            value = jnp.minimum(jnp.maximum(springs[k] + mods[k] * inc, -lim), lim)
            springs[k] = value
            stress = stress + value
        edge[pl.ds(s, 1), :] = stress[55:56]
        above = jnp.where(row == 0, 0.0, pltpu.roll(stress, 1, 0))
        vel = vel + stress_rate * (stress - above)
        return disp + vel, vel, strain

    zero = jnp.zeros((64, 128), F32)
    out[...] = lax.fori_loop(0, STEPS, step, (start[...], zero, zero))[0]


def last_rows_kernel(count, modulus, yields, soil, start, edge, arrived, done, out):
    del done
    row = lax.broadcasted_iota(jnp.int32, (8, 128), 0)
    for t in range(4):
        cols = slice(t * 128, (t + 1) * 128)
        base = arrived[0, t * 8 : t * 8 + 8]
        for source in range(1, arrived.shape[0]):
            base = base + arrived[source, t * 8 : t * 8 + 8]
        cls = soil[:, cols]
        pairs = [spring_values(cls, k, count, modulus, yields) for k in range(16)]
        springs = [jnp.zeros((8, 128), F32) for _ in range(16)]
        disp = start[:, cols]
        vel = jnp.zeros((8, 128), F32)
        old = jnp.zeros((8, 128), F32)
        for s in range(STEPS):
            strain = jnp.where(row == 7, base[s : s + 1], pltpu.roll(disp, 7, 0)) - disp
            inc = strain - old
            old = strain
            for k in range(16):
                mod, lim = pairs[k]
                springs[k] = jnp.minimum(jnp.maximum(springs[k] + mod * inc, -lim), lim)
            sums = springs
            while len(sums) > 1:
                sums = [sums[i] + sums[i + 1] for i in range(0, len(sums), 2)]
            stress = sums[0]
            above = jnp.where(row == 0, edge[s : s + 1, cols], pltpu.roll(stress, 1, 0))
            vel = vel + stress_rate * (stress - above)
            disp = disp + vel
        out[:, cols] = disp


RIGHT = ((8, 8, 0), (9, 7, 8), (9, 7, 15))
LEFT = ((0, 8, 0), (0, 7, 8), (0, 7, 15))


def run_copies(pairs, sems):
    copies = [pltpu.make_async_copy(src, dst, sems.at[n]) for n, (src, dst) in enumerate(pairs)]
    for copy in copies:
        copy.start()
    for copy in copies:
        copy.wait()


def pack_x_kernel(u, p, c, edge_right, edge_left, mid_right, mid_left, sems):
    pairs = []
    for plan, edge, mid in ((RIGHT, edge_right, mid_right), (LEFT, edge_left, mid_left)):
        for ref, (x0, n, at) in zip((u, p, c), plan):
            pairs.append((ref.at[x0 : x0 + n, 0:8, :], edge.at[at : at + n, 0:8, :]))
            pairs.append((ref.at[x0 : x0 + n, 56:64, :], edge.at[at : at + n, 8:16, :]))
            pairs.append((ref.at[x0 : x0 + n, 8:56, :], mid.at[at : at + n, :, :]))
    run_copies(pairs, sems)


def pack_y_kernel(u, p, c, from_left, from_right, send_a, send_b, sems):
    odd = lax.rem(lax.axis_index("gy"), 2)
    pairs = []
    for send, side in ((send_a, 1 - odd), (send_b, odd)):
        own = pl.ds(pl.multiple_of(side * 56, 8), 8)
        corner = pl.ds(pl.multiple_of(side * 8, 8), 8)
        for n, ref in enumerate((u, p, c)):
            pairs.append((ref.at[:, own, :], send.at[16 * n : 16 * n + 16]))
        pairs.append((from_left.at[:, corner, :], send.at[48:70]))
        pairs.append((from_right.at[:, corner, :], send.at[70:92]))
    run_copies(pairs, sems)


def region_kernel(u, p, c, el, er, ml, mr, ya, yb, out, one, two, coef, sems):
    low_x, high_x = x_edges()
    low_y, high_y = y_edges()
    even = lax.rem(lax.axis_index("gy"), 2) == 0
    bufs = (one, two, coef)
    always = jnp.bool_(True)
    jobs = []

    def job(cond, src, dst):
        jobs.append((cond, pltpu.make_async_copy(src, dst, sems.at[len(jobs)])))

    for ref, buf in zip((u, p, c), bufs):
        job(None, ref, buf.at[0:16, 16:80, :])
    left_at = ((24, 8, 0), (25, 7, 8), (25, 7, 15))
    right_at = ((16, 8, 0), (16, 7, 8), (16, 7, 15))
    for cond, plan, edge, mid in ((~low_x, left_at, el, ml), (~high_x, right_at, er, mr)):
        for buf, (x0, n, at) in zip(bufs, plan):
            job(cond, mid.at[at : at + n], buf.at[x0 : x0 + n, 24:72, :])
            job(cond, edge.at[at : at + n, 0:8, :], buf.at[x0 : x0 + n, 16:24, :])
            job(cond, edge.at[at : at + n, 8:16, :], buf.at[x0 : x0 + n, 72:80, :])
    for msg, is_high in ((ya, even), (yb, ~even)):
        for rows, cond in (((80, 88), is_high & ~high_y), ((8, 16), ~is_high & ~low_y)):
            for n, buf in enumerate(bufs):
                job(cond, msg.at[16 * n : 16 * n + 16], buf.at[0:16, rows[0] : rows[1], :])
            for more, plan, base in ((~low_x, left_at, 48), (~high_x, right_at, 70)):
                for buf, (x0, n, at) in zip(bufs, plan):
                    job(
                        cond & more,
                        msg.at[base + at : base + at + n],
                        buf.at[x0 : x0 + n, rows[0] : rows[1], :],
                    )
    for cond, copy in jobs:
        if cond is None:
            copy.start()
        else:
            pl.when(cond)(copy.start)
    for edge, x0, n, y0, m in (
        (low_x, 24, 8, 8, 80),
        (high_x, 16, 8, 8, 80),
        (low_y, 0, 32, 8, 8),
        (high_y, 0, 32, 80, 8),
    ):

        @pl.when(edge)
        def _():
            for buf in bufs:
                buf[x0 : x0 + n, y0 : y0 + m, :] = jnp.zeros((n, m, 256), F32)

    for cond, copy in jobs:
        if cond is None:
            copy.wait()
        else:
            pl.when(cond)(copy.wait)

    now, old = one, two
    for step in range(1, STEPS + 1):
        last = step == STEPS
        y0, rows = (16, 64) if last else (8, 80)
        lane = lanes((rows, 128))
        top, end = lane == 0, lane == 127

        def row(i, carry, now=now, old=old, step=step, y0=y0, rows=rows, top=top, end=end, last=last):
            x = i + (step - HALO)
            at, lower, upper = (x + 32) & 31, (x + 31) & 31, (x + 33) & 31
            here = slice(y0, y0 + rows)
            halves = (slice(0, 128), slice(128, 256))
            a, b = (now[at, here, h] for h in halves)
            ra, rb = pltpu.roll(a, 1, 1), pltpu.roll(b, 1, 1)
            la, lb = pltpu.roll(a, 127, 1), pltpu.roll(b, 127, 1)
            depth = (
                jnp.where(top, a, ra) + jnp.where(end, lb, la),
                jnp.where(top, ra, rb) + jnp.where(end, 0.0, lb),
            )
            for h, v, dz in zip(halves, (a, b), depth):
                beside = now[lower, here, h] + now[upper, here, h]
                beside = beside + (now[at, y0 - 1 : y0 - 1 + rows, h] + now[at, y0 + 1 : y0 + 1 + rows, h])
                lap = beside + dz - 6.0 * v
                value = (2.0 * v - old[at, here, h]) + coef[at, here, h] * lap
                if last:
                    out[x, :, h] = value
                else:
                    old[at, here, h] = value
            return carry

        lax.fori_loop(0, 32 - 2 * step, row, 0)
        now, old = old, now


def shards(
    reg_disp,
    reg_prev,
    reg_coef,
    basin_disp,
    face_index,
    soil_class,
    spring_count,
    spring_modulus,
    spring_yield,
):
    n_gx = lax.axis_size("gx")
    n_x = lax.axis_size("sec") * n_gx
    right = [(i, (i + 1) % n_x) for i in range(n_x)]
    left = [(i, (i - 1) % n_x) for i in range(n_x)]
    swap_a = [(0, 1), (1, 0), (2, 3), (3, 2)]
    swap_b = [(0, 0), (1, 2), (2, 1), (3, 3)]
    regional = (reg_disp, reg_prev, reg_coef)

    half = pl.BlockSpec((16, 64, 128), lambda i: (0, 0, 0))
    whole = lambda *s: pl.BlockSpec(s, lambda i: (0,) * len(s))
    band, band_right, band_left = pl.pallas_call(
        band_kernel,
        grid=(1,),
        out_shape=(sds(48, 8, 128), sds(24, 8, 128), sds(24, 8, 128)),
        in_specs=[half] * 3,
        out_specs=(whole(48, 8, 128), whole(24, 8, 128), whole(24, 8, 128)),
        compiler_params=PARAMS,
        name="band",
    )(*regional)
    band_from_left = lax.ppermute(band_right, XAX, right)
    band_from_right = lax.ppermute(band_left, XAX, left)

    edge_right, edge_left, mid_right, mid_left = pl.pallas_call(
        pack_x_kernel,
        out_shape=(sds(22, 16, 256), sds(22, 16, 256), sds(22, 48, 256), sds(22, 48, 256)),
        in_specs=[ANY] * 3,
        out_specs=(ANY,) * 4,
        scratch_shapes=[pltpu.SemaphoreType.DMA((18,))],
        compiler_params=PARAMS,
        name="pack_x",
    )(*regional)
    edge_from_left = lax.ppermute(edge_right, XAX, right)
    edge_from_right = lax.ppermute(edge_left, XAX, left)
    mid_from_left = lax.ppermute(mid_right, XAX, right)
    mid_from_right = lax.ppermute(mid_left, XAX, left)

    ext, band_a, band_b = pl.pallas_call(
        band_edges_kernel,
        out_shape=(sds(48, 32, 128), sds(3, 32, 128), sds(3, 32, 128)),
        in_specs=[VM] * 3,
        out_specs=(VM,) * 3,
        compiler_params=PARAMS,
        name="band_edges",
    )(band, band_from_left, band_from_right)
    band_a = lax.ppermute(band_a, "gy", swap_a)
    band_b = lax.ppermute(band_b, "gy", swap_b)
    trace = pl.pallas_call(
        band_steps_kernel,
        out_shape=sds(8, 8, 128),
        in_specs=[VM] * 3,
        out_specs=VM,
        scratch_shapes=[pltpu.VMEM((17, 32, 128), F32)] * 3,
        compiler_params=PARAMS,
        name="band_steps",
    )(ext, band_a, band_b)

    table = lax.all_gather(trace, "gy").reshape(32, 8, 128)
    index = lax.all_gather(face_index.reshape(4, 128), "gx").reshape(n_gx * 4, 128)
    picked = pl.pallas_call(
        pick_kernel,
        out_shape=sds(n_gx * 4, 8, 128),
        in_specs=[VM] * 2,
        out_specs=VM,
        compiler_params=PARAMS,
        name="pick",
    )(table, index)
    arrived = lax.all_to_all(picked.reshape(n_gx, 32, 128), "gx", 0, 0)

    y_a, y_b = pl.pallas_call(
        pack_y_kernel,
        out_shape=(sds(92, 8, 256), sds(92, 8, 256)),
        in_specs=[ANY] * 5,
        out_specs=(ANY,) * 2,
        scratch_shapes=[pltpu.SemaphoreType.DMA((10,))],
        compiler_params=PARAMS,
        name="pack_y",
    )(*regional, edge_from_left, edge_from_right)
    y_a = lax.ppermute(y_a, "gy", swap_a)
    y_b = lax.ppermute(y_b, "gy", swap_b)

    soil = soil_class[0]
    start = basin_disp[0]
    tables = (spring_count, spring_modulus, spring_yield)
    block = pl.BlockSpec((64, 128), lambda i: (0, i))
    upper, edge = pl.pallas_call(
        columns_kernel,
        grid=(4,),
        out_shape=(sds(64, 512), sds(8, 512)),
        in_specs=[SM] * 3 + [block] * 2,
        out_specs=(block, pl.BlockSpec((8, 128), lambda i: (0, i))),
        scratch_shapes=[pltpu.VMEM((16, 64, 128), F32)] * 3,
        compiler_params=PARAMS,
        name="columns",
    )(*tables, soil, start)

    tail = pl.BlockSpec((8, 512), lambda i: (7, 0))
    basin = pl.pallas_call(
        last_rows_kernel,
        grid=(1,),
        out_shape=sds(64, 512),
        in_specs=[SM] * 3 + [tail, tail, whole(8, 512), whole(n_gx, 32, 128), ANY],
        out_specs=tail,
        input_output_aliases={7: 0},
        compiler_params=PARAMS,
        name="last_rows",
    )(*tables, soil, start, edge, arrived, upper)

    final = pl.pallas_call(
        region_kernel,
        out_shape=sds(16, 64, 256),
        in_specs=[ANY] * 9,
        out_specs=VM,
        scratch_shapes=[pltpu.VMEM((32, 96, 256), F32)] * 3 + [pltpu.SemaphoreType.DMA((64,))],
        compiler_params=PARAMS,
        name="region",
    )(*regional, edge_from_left, edge_from_right, mid_from_left, mid_from_right, y_a, y_b)
    return (final, basin[None])


def solution(mesh):
    in_specs = (
        P(("sec", "gx"), "gy", None),
        P(("sec", "gx"), "gy", None),
        P(("sec", "gx"), "gy", None),
        P("sec", None, ("gx", "gy")),
        P("sec", ("gx", "gy")),
        P("sec", None, ("gx", "gy")),
        P(),
        P(),
        P(),
    )
    out_specs = (P(("sec", "gx"), "gy", None), P("sec", None, ("gx", "gy")))
    return jax.shard_map(shards, mesh=mesh, in_specs=in_specs, out_specs=out_specs, check_vma=False)
```

```python
import functools
import jax
import jax.numpy as jnp
from jax import lax
from jax.experimental import pallas as pl
from jax.experimental.pallas import tpu as pltpu
from jax.sharding import PartitionSpec as P

STEPS = 8
HALO = 8
FDEP = 64
stress_rate = 0.5
XAX = ("sec", "gx")
ALL = ("sec", "gx", "gy")
F32 = jnp.float32
ANY = pl.BlockSpec(memory_space=pl.ANY)
VM = pl.BlockSpec(memory_space=pltpu.VMEM)
SM = pl.BlockSpec(memory_space=pltpu.SMEM)
PARAMS = pltpu.CompilerParams(vmem_limit_bytes=40 * 1024 * 1024)
LARGE = pltpu.CompilerParams(vmem_limit_bytes=60 * 1024 * 1024)


def sds(*shape):
    return jax.ShapeDtypeStruct(shape, F32)


def x_edges():
    at = lax.axis_index("sec") * lax.axis_size("gx") + lax.axis_index("gx")
    return at == 0, at == lax.axis_size("sec") * lax.axis_size("gx") - 1


def y_edges():
    at = lax.axis_index("gy")
    return at == 0, at == lax.axis_size("gy") - 1


def lanes(shape):
    return lax.broadcasted_iota(jnp.int32, shape, len(shape) - 1)


def band_kernel(u, p, c, band, to_right, to_left):
    lane = lanes((64, 128))
    for x in range(8):
        halves = []
        for row in (x, x + 8):
            halves.append(
                jnp.where(
                    lane < 73,
                    u[row],
                    jnp.where(lane < 88, pltpu.roll(p[row], 16, 1), pltpu.roll(c[row], 31, 1)),
                )
            )
        turned = jnp.concatenate(halves, axis=0).T
        band[:, x, :] = turned[56:104]
    first = lanes((8, 128)) < 64
    for k in range(24):
        a, b = band[k], band[k + 24]
        ra, rb = pltpu.roll(a, 64, 1), pltpu.roll(b, 64, 1)
        to_right[k] = jnp.where(first, ra, b)
        to_left[k] = jnp.where(first, a, rb)


def band_edges_kernel(band, from_left, from_right, ext, send_a, send_b):
    low_edge, high_edge = x_edges()
    even = lax.rem(lax.axis_index("gy"), 2) == 0
    lane = lanes((8, 128))
    first = lane < 64
    group = lanes((32, 128)) // 8
    for g in range(3):
        high = jnp.zeros((32, 128), F32)
        low = jnp.zeros((32, 128), F32)
        for q in range(16):
            level = g * 16 + q
            own = band[level]
            near = from_right[level % 24]
            far = from_left[level % 24]
            if level >= 24:
                near, far = pltpu.roll(near, 64, 1), pltpu.roll(far, 64, 1)
            near = jnp.where(high_edge, 0.0, near)
            far = jnp.where(low_edge, 0.0, far)
            full = jnp.concatenate([own, pltpu.roll(own, 64, 1), near, far], axis=0)
            ext[level] = full
            high = jnp.where(group == q, pltpu.roll(full, (q * 8 - 56) % 128, 1), high)
            low = jnp.where(group == q, pltpu.roll(full, q * 8, 1), low)
        send_a[g] = jnp.where(even, high, low)
        send_b[g] = jnp.where(even, low, high)


def band_steps_kernel(ext, recv_a, recv_b, trace, one, two, coef):
    low_edge, high_edge = y_edges()
    even = lax.rem(lax.axis_index("gy"), 2) == 0
    lane = lanes((32, 128))
    for g in range(3):
        a, b = recv_a[g], recv_b[g]
        high = jnp.where(high_edge, 0.0, jnp.where(even, a, b))
        low = jnp.where(low_edge, 0.0, jnp.where(even, b, a))
        for q in range(16):
            level = g * 16 + q
            if level > 46:
                continue
            full = jnp.where(
                lane < 64,
                ext[level],
                jnp.where(
                    lane < 72,
                    pltpu.roll(high, (64 - q * 8) % 128, 1),
                    jnp.where(lane >= 120, pltpu.roll(low, (120 - q * 8) % 128, 1), 0.0),
                ),
            )
            if level < 17:
                one[level] = full
            elif level < 32:
                two[level - 16] = full
            else:
                coef[level - 31] = full
    first = lanes((8, 128)) < 64
    now, old = one, two
    for step in range(1, STEPS + 1):
        for j in range(step, 17 - step):
            u = now[j]
            beside = pltpu.roll(u, 1, 0) + pltpu.roll(u, 31, 0) + pltpu.roll(u, 1, 1) + pltpu.roll(u, 127, 1)
            lap = beside + now[j - 1] + now[j + 1] - 6.0 * u
            old[j] = 2.0 * u - old[j] + coef[j] * lap
        now, old = old, now
        plane = now[8]
        trace[:, step - 1, :] = jnp.where(first, plane[0:8], pltpu.roll(plane[8:16], 64, 1))


def pick_kernel(table, index, out):
    me = lax.axis_index("gy")
    count = table.shape[0]

    def tile(t):
        cell = jnp.broadcast_to(index[pl.ds(t, 1), :], (8, 128))
        x, y = cell >> 8, cell & 255
        place = ((x >> 4) << 3) + (x & 7)
        place = jnp.where((y >> 6) == me, place, -1)
        lane = (((x >> 3) & 1) << 6) + (y & 63)
        accs = [jnp.zeros((8, 128), F32) for _ in range(4)]
        for k in range(count):
            found = jnp.take_along_axis(table[k], lane, axis=1)
            accs[k % 4] = jnp.where(place == k, found, accs[k % 4])
        out[t] = (accs[0] + accs[1]) + (accs[2] + accs[3])

    def tiles(i, carry):
        for t in range(2):
            tile(i * 2 + t)
        return carry

    lax.fori_loop(0, index.shape[0] // 2, tiles, 0)


def spring_values(cls, k, count, modulus, yields):
    mod = jnp.zeros(cls.shape, F32)
    lim = jnp.zeros(cls.shape, F32)
    for c in range(8):
        hit = cls == c
        mod = jnp.where(hit, modulus[c, k], mod)
        lim = jnp.where(hit, jnp.where(k < count[c], yields[c, k], 0.0), lim)
    return mod, lim


def columns_kernel(count, modulus, yields, soil, start, out, edge, mods, lims, springs):
    width = soil.shape[1]

    def rows(r, carry):
        at = pl.ds(pl.multiple_of(r * 8, 8), 8)
        cls = soil[at, :]
        for k in range(16):
            mod, lim = spring_values(cls, k, count, modulus, yields)
            mods[k, at, :] = mod
            lims[k, at, :] = lim
            springs[k, at, :] = jnp.zeros((8, width), F32)
        return carry

    lax.fori_loop(0, 8, rows, 0)
    row = lax.broadcasted_iota(jnp.int32, (64, width), 0)

    def step(s, state):
        disp, vel, old = state
        strain = pltpu.roll(disp, 63, 0) - disp
        inc = strain - old
        parts = []
        for r in range(0, 64, 16):
            here = slice(r, r + 16)
            change = inc[here]
            stress = jnp.zeros((16, width), F32)
            for k in range(16):
                lim = lims[k, here, :]
                value = jnp.minimum(jnp.maximum(springs[k, here, :] + mods[k, here, :] * change, -lim), lim)
                springs[k, here, :] = value
                stress = stress + value
            parts.append(stress)
        stress = jnp.concatenate(parts, axis=0)
        edge[pl.ds(s, 1), :] = stress[55:56]
        above = jnp.where(row == 0, 0.0, pltpu.roll(stress, 1, 0))
        vel = vel + stress_rate * (stress - above)
        return disp + vel, vel, strain

    zero = jnp.zeros((64, width), F32)
    out[...] = lax.fori_loop(0, STEPS, step, (start[...], zero, zero))[0]


def last_rows_kernel(count, modulus, yields, soil, start, edge, arrived, done, out):
    del done
    row = lax.broadcasted_iota(jnp.int32, (8, 128), 0)
    for t in range(4):
        cols = slice(t * 128, (t + 1) * 128)
        base = arrived[0, t * 8 : t * 8 + 8]
        for source in range(1, arrived.shape[0]):
            base = base + arrived[source, t * 8 : t * 8 + 8]
        cls = soil[:, cols]
        pairs = [spring_values(cls, k, count, modulus, yields) for k in range(16)]
        springs = [jnp.zeros((8, 128), F32) for _ in range(16)]
        disp = start[:, cols]
        vel = jnp.zeros((8, 128), F32)
        old = jnp.zeros((8, 128), F32)
        for s in range(STEPS):
            strain = jnp.where(row == 7, base[s : s + 1], pltpu.roll(disp, 7, 0)) - disp
            inc = strain - old
            old = strain
            for k in range(16):
                mod, lim = pairs[k]
                springs[k] = jnp.minimum(jnp.maximum(springs[k] + mod * inc, -lim), lim)
            sums = springs
            while len(sums) > 1:
                sums = [sums[i] + sums[i + 1] for i in range(0, len(sums), 2)]
            stress = sums[0]
            above = jnp.where(row == 0, edge[s : s + 1, cols], pltpu.roll(stress, 1, 0))
            vel = vel + stress_rate * (stress - above)
            disp = disp + vel
        out[:, cols] = disp


RIGHT = ((8, 8, 0), (9, 7, 8), (9, 7, 15))
LEFT = ((0, 8, 0), (0, 7, 8), (0, 7, 15))


def start_jobs(jobs, sems):
    copies = [(cond, pltpu.make_async_copy(src, dst, sems.at[n])) for n, (cond, src, dst) in enumerate(jobs)]
    for cond, copy in copies:
        if cond is None:
            copy.start()
        else:
            pl.when(cond)(copy.start)
    return copies


def wait_jobs(copies):
    for cond, copy in copies:
        if cond is None:
            copy.wait()
        else:
            pl.when(cond)(copy.wait)


def run_jobs(jobs, sems):
    wait_jobs(start_jobs(jobs, sems))


def pack_x_kernel(u, p, c, edge_right, edge_left, mid_right, mid_left, mid_far, sems):
    jobs = []
    gx = lax.axis_index("gx")
    for plan, edge, mid, ends in (
        (RIGHT, edge_right, mid_right, gx == lax.axis_size("gx") - 1),
        (LEFT, edge_left, mid_left, gx == 0),
    ):
        for ref, (x0, n, at) in zip((u, p, c), plan):
            middle = ref.at[x0 : x0 + n, 8:56, :]
            jobs.append((None, ref.at[x0 : x0 + n, 0:8, :], edge.at[at : at + n, 0:8, :]))
            jobs.append((None, ref.at[x0 : x0 + n, 56:64, :], edge.at[at : at + n, 8:16, :]))
            jobs.append((None, middle, mid.at[at : at + n, :, :]))
            jobs.append((ends, middle, mid_far.at[at : at + n, :, :]))
    run_jobs(jobs, sems)


def pack_y_kernel(u, p, c, from_left, from_right, send_a, send_b, sems):
    odd = lax.rem(lax.axis_index("gy"), 2)
    pairs = []
    for send, side in ((send_a, 1 - odd), (send_b, odd)):
        own = pl.ds(pl.multiple_of(side * 56, 8), 8)
        corner = pl.ds(pl.multiple_of(side * 8, 8), 8)
        for n, ref in enumerate((u, p, c)):
            pairs.append((None, ref.at[:, own, :], send.at[16 * n : 16 * n + 16]))
        pairs.append((None, from_left.at[:, corner, :], send.at[48:70]))
        pairs.append((None, from_right.at[:, corner, :], send.at[70:92]))
    run_jobs(pairs, sems)


def region_kernel(u, p, c, el, er, ml, mr, relayed, ya, yb, out, one, two, coef, sems):
    low_x, high_x = x_edges()
    low_y, high_y = y_edges()
    even = lax.rem(lax.axis_index("gy"), 2) == 0
    bufs = (one, two, coef)
    gx = lax.axis_index("gx")
    first, final = gx == 0, gx == lax.axis_size("gx") - 1
    jobs = []

    def job(cond, src, dst):
        jobs.append((cond, src, dst))

    for ref, buf in zip((u, p, c), bufs):
        job(None, ref, buf.at[0:16, 16:80, :])
    left_at = ((24, 8, 0), (25, 7, 8), (25, 7, 15))
    right_at = ((16, 8, 0), (16, 7, 8), (16, 7, 15))
    for cond, far, plan, edge, mid in ((~low_x, first, left_at, el, ml), (~high_x, final, right_at, er, mr)):
        for buf, (x0, n, at) in zip(bufs, plan):
            job(~far, mid.at[at : at + n], buf.at[x0 : x0 + n, 24:72, :])
            job(far & cond, relayed.at[at : at + n], buf.at[x0 : x0 + n, 24:72, :])
            job(cond, edge.at[at : at + n, 0:8, :], buf.at[x0 : x0 + n, 16:24, :])
            job(cond, edge.at[at : at + n, 8:16, :], buf.at[x0 : x0 + n, 72:80, :])
    for msg, is_high in ((ya, even), (yb, ~even)):
        for rows, cond in (((80, 88), is_high & ~high_y), ((8, 16), ~is_high & ~low_y)):
            for n, buf in enumerate(bufs):
                job(cond, msg.at[16 * n : 16 * n + 16], buf.at[0:16, rows[0] : rows[1], :])
            for more, plan, base in ((~low_x, left_at, 48), (~high_x, right_at, 70)):
                for buf, (x0, n, at) in zip(bufs, plan):
                    job(
                        cond & more,
                        msg.at[base + at : base + at + n],
                        buf.at[x0 : x0 + n, rows[0] : rows[1], :],
                    )
    copies = start_jobs(jobs, sems)
    for edge, x0, n, y0, m in (
        (low_x, 24, 8, 8, 80),
        (high_x, 16, 8, 8, 80),
        (low_y, 0, 32, 8, 8),
        (high_y, 0, 32, 80, 8),
    ):

        @pl.when(edge)
        def _():
            for buf in bufs:
                buf[x0 : x0 + n, y0 : y0 + m, :] = jnp.zeros((n, m, 256), F32)

    wait_jobs(copies)

    now, old = one, two
    halves = (slice(0, 128), slice(128, 256))
    rows = 16
    lane = lanes((rows, 128))
    top, end = lane == 0, lane == 127
    for step in range(1, STEPS + 1):
        last = step == STEPS
        for x in range(step - HALO, 16 + HALO - step):
            at, lower, upper = x % 32, (x - 1) % 32, (x + 1) % 32
            for y0 in range(16, 80, rows) if last else range(8, 88, rows):
                here = slice(y0, y0 + rows)
                a, b = (now[at, here, h] for h in halves)
                ra, rb = pltpu.roll(a, 1, 1), pltpu.roll(b, 1, 1)
                la, lb = pltpu.roll(a, 127, 1), pltpu.roll(b, 127, 1)
                depth = (
                    jnp.where(top, a, ra) + jnp.where(end, lb, la),
                    jnp.where(top, ra, rb) + jnp.where(end, 0.0, lb),
                )
                for h, v, dz in zip(halves, (a, b), depth):
                    beside = now[lower, here, h] + now[upper, here, h]
                    beside = beside + (now[at, y0 - 1 : y0 - 1 + rows, h] + now[at, y0 + 1 : y0 + 1 + rows, h])
                    lap = beside + dz - 6.0 * v
                    value = (2.0 * v - old[at, here, h]) + coef[at, here, h] * lap
                    if last:
                        out[x, y0 - 16 : y0 - 16 + rows, h] = value
                    else:
                        old[at, here, h] = value
        now, old = old, now


def relays(n_sec, n_gx):
    def at(sec, gx, gy):
        return (sec % n_sec * n_gx + gx) * 4 + gy

    top = n_gx - 1
    out, into = [], []
    for sec in range(n_sec):
        for gy in range(4):
            up, down = ((3, 12), (11, 4))[gy % 2]
            out += [(at(sec, top, gy), at(sec, up, gy)), (at(sec, 0, gy), at(sec, down, gy))]
            if sec < n_sec - 1:
                into.append((at(sec, up, gy), at(sec + 1, 0, gy)))
            if sec > 0:
                into.append((at(sec, down, gy), at(sec - 1, top, gy)))
    return out, into


def shards(
    reg_disp,
    reg_prev,
    reg_coef,
    basin_disp,
    face_index,
    soil_class,
    spring_count,
    spring_modulus,
    spring_yield,
):
    n_gx = lax.axis_size("gx")
    n_x = lax.axis_size("sec") * n_gx
    right = [(i, (i + 1) % n_x) for i in range(n_x)]
    left = [(i, (i - 1) % n_x) for i in range(n_x)]
    swap_a = [(0, 1), (1, 0), (2, 3), (3, 2)]
    swap_b = [(0, 0), (1, 2), (2, 1), (3, 3)]
    regional = (reg_disp, reg_prev, reg_coef)
    half = pl.BlockSpec((16, 64, 128), lambda i: (0, 0, 0))
    whole = lambda *s: pl.BlockSpec(s, lambda i: (0,) * len(s))
    band, band_right, band_left = pl.pallas_call(
        band_kernel,
        grid=(1,),
        out_shape=(sds(48, 8, 128), sds(24, 8, 128), sds(24, 8, 128)),
        in_specs=[half] * 3,
        out_specs=(whole(48, 8, 128), whole(24, 8, 128), whole(24, 8, 128)),
        compiler_params=LARGE,
        name="band",
    )(*regional)
    band_from_left = lax.ppermute(band_right, XAX, right)
    band_from_right = lax.ppermute(band_left, XAX, left)
    index, _ = lax.optimization_barrier((face_index.reshape(1, 4, 128), band_right))
    index = lax.all_gather(index, "gy").reshape(16, 128)

    regional, index = lax.optimization_barrier((regional, index))
    edge_right, edge_left, mid_right, mid_left, mid_far = pl.pallas_call(
        pack_x_kernel,
        out_shape=(sds(22, 16, 256), sds(22, 16, 256), sds(22, 48, 256), sds(22, 48, 256), sds(22, 48, 256)),
        in_specs=[ANY] * 3,
        out_specs=(ANY,) * 5,
        scratch_shapes=[pltpu.SemaphoreType.DMA((24,))],
        compiler_params=PARAMS,
        name="pack_x",
    )(*regional)
    edge_from_left = lax.ppermute(edge_right, XAX, right)
    edge_from_right = lax.ppermute(edge_left, XAX, left)
    relay_out, relay_in = relays(lax.axis_size("sec"), n_gx)
    mid_relay = lax.ppermute(mid_far, ALL, relay_out)
    mid_from_left = lax.ppermute(mid_right, "gx", [(i, i + 1) for i in range(n_gx - 1)])
    mid_from_right = lax.ppermute(mid_left, "gx", [(i + 1, i) for i in range(n_gx - 1)])
    mid_relay = lax.ppermute(mid_relay, ALL, relay_in)

    ext, band_a, band_b = pl.pallas_call(
        band_edges_kernel,
        out_shape=(sds(48, 32, 128), sds(3, 32, 128), sds(3, 32, 128)),
        in_specs=[VM] * 3,
        out_specs=(VM,) * 3,
        compiler_params=PARAMS,
        name="band_edges",
    )(band, band_from_left, band_from_right)
    band_a = lax.ppermute(band_a, "gy", swap_a)
    band_b = lax.ppermute(band_b, "gy", swap_b)
    trace = pl.pallas_call(
        band_steps_kernel,
        out_shape=sds(8, 8, 128),
        in_specs=[VM] * 3,
        out_specs=VM,
        scratch_shapes=[pltpu.VMEM((17, 32, 128), F32)] * 3,
        compiler_params=PARAMS,
        name="band_steps",
    )(ext, band_a, band_b)

    table = lax.all_to_all(jnp.broadcast_to(trace.reshape(1, 64, 128), (n_gx, 64, 128)), "gx", 0, 0)
    table = table.reshape(n_gx * 8, 8, 128)
    picked = pl.pallas_call(
        pick_kernel,
        out_shape=sds(16, 8, 128),
        in_specs=[VM] * 2,
        out_specs=VM,
        compiler_params=PARAMS,
        name="pick",
    )(table, index)
    arrived = lax.all_to_all(picked.reshape(4, 32, 128), "gy", 0, 0)

    y_a, y_b = pl.pallas_call(
        pack_y_kernel,
        out_shape=(sds(92, 8, 256), sds(92, 8, 256)),
        in_specs=[ANY] * 5,
        out_specs=(ANY,) * 2,
        scratch_shapes=[pltpu.SemaphoreType.DMA((10,))],
        compiler_params=PARAMS,
        name="pack_y",
    )(*regional, edge_from_left, edge_from_right)
    y_a = lax.ppermute(y_a, "gy", swap_a)
    y_b = lax.ppermute(y_b, "gy", swap_b)

    soil = soil_class[0]
    start = basin_disp[0]
    tables = (spring_count, spring_modulus, spring_yield)
    block = pl.BlockSpec((64, 256), lambda i: (0, i))
    upper, edge = pl.pallas_call(
        columns_kernel,
        grid=(2,),
        out_shape=(sds(64, 512), sds(8, 512)),
        in_specs=[SM] * 3 + [block] * 2,
        out_specs=(block, pl.BlockSpec((8, 256), lambda i: (0, i))),
        scratch_shapes=[pltpu.VMEM((16, 64, 256), F32)] * 3,
        compiler_params=PARAMS,
        name="columns",
    )(*tables, soil, start)

    tail = pl.BlockSpec((8, 512), lambda i: (7, 0))
    basin = pl.pallas_call(
        last_rows_kernel,
        grid=(1,),
        out_shape=sds(64, 512),
        in_specs=[SM] * 3 + [tail, tail, whole(8, 512), whole(4, 32, 128), ANY],
        out_specs=tail,
        input_output_aliases={7: 0},
        compiler_params=PARAMS,
        name="last_rows",
    )(*tables, soil, start, edge, arrived, upper)

    final = pl.pallas_call(
        region_kernel,
        out_shape=sds(16, 64, 256),
        in_specs=[ANY] * 10,
        out_specs=VM,
        scratch_shapes=[pltpu.VMEM((32, 96, 256), F32)] * 3 + [pltpu.SemaphoreType.DMA((64,))],
        compiler_params=PARAMS,
        name="region",
    )(*regional, edge_from_left, edge_from_right, mid_from_left, mid_from_right, mid_relay, y_a, y_b)
    return (final, basin[None])


def solution(mesh):
    in_specs = (
        P(("sec", "gx"), "gy", None),
        P(("sec", "gx"), "gy", None),
        P(("sec", "gx"), "gy", None),
        P("sec", None, ("gx", "gy")),
        P("sec", ("gx", "gy")),
        P("sec", None, ("gx", "gy")),
        P(),
        P(),
        P(),
    )
    out_specs = (P(("sec", "gx"), "gy", None), P("sec", None, ("gx", "gy")))
    return jax.shard_map(shards, mesh=mesh, in_specs=in_specs, out_specs=out_specs, check_vma=False)
```

```python
import functools
import jax
import jax.numpy as jnp
from jax import lax
from jax.experimental import pallas as pl
from jax.experimental.pallas import tpu as pltpu
from jax.sharding import PartitionSpec as P

STEPS = 8
HALO = 8
FDEP = 64
stress_rate = 0.5
XAX = ("sec", "gx")
ALL = ("sec", "gx", "gy")
F32 = jnp.float32
ANY = pl.BlockSpec(memory_space=pl.ANY)
VM = pl.BlockSpec(memory_space=pltpu.VMEM)
SM = pl.BlockSpec(memory_space=pltpu.SMEM)
PARAMS = pltpu.CompilerParams(vmem_limit_bytes=40 * 1024 * 1024)
LARGE = pltpu.CompilerParams(vmem_limit_bytes=60 * 1024 * 1024)


def sds(*shape):
    return jax.ShapeDtypeStruct(shape, F32)


def x_edges():
    at = lax.axis_index("sec") * lax.axis_size("gx") + lax.axis_index("gx")
    return at == 0, at == lax.axis_size("sec") * lax.axis_size("gx") - 1


def y_edges():
    at = lax.axis_index("gy")
    return at == 0, at == lax.axis_size("gy") - 1


def lanes(shape):
    return lax.broadcasted_iota(jnp.int32, shape, len(shape) - 1)


def band_kernel(u, p, c, band, to_right, to_left):
    lane = lanes((64, 128))
    for x in range(8):
        halves = []
        for row in (x, x + 8):
            halves.append(
                jnp.where(
                    lane < 73,
                    u[row],
                    jnp.where(lane < 88, pltpu.roll(p[row], 16, 1), pltpu.roll(c[row], 31, 1)),
                )
            )
        turned = jnp.concatenate(halves, axis=0).T
        band[:, x, :] = turned[56:104]
    first = lanes((8, 128)) < 64
    for k in range(24):
        a, b = band[k], band[k + 24]
        ra, rb = pltpu.roll(a, 64, 1), pltpu.roll(b, 64, 1)
        to_right[k] = jnp.where(first, ra, b)
        to_left[k] = jnp.where(first, a, rb)


def band_edges_kernel(band, from_left, from_right, ext, send_a, send_b):
    low_edge, high_edge = x_edges()
    even = lax.rem(lax.axis_index("gy"), 2) == 0
    lane = lanes((8, 128))
    first = lane < 64
    group = lanes((32, 128)) // 8
    for g in range(3):
        high = jnp.zeros((32, 128), F32)
        low = jnp.zeros((32, 128), F32)
        for q in range(16):
            level = g * 16 + q
            own = band[level]
            near = from_right[level % 24]
            far = from_left[level % 24]
            if level >= 24:
                near, far = pltpu.roll(near, 64, 1), pltpu.roll(far, 64, 1)
            near = jnp.where(high_edge, 0.0, near)
            far = jnp.where(low_edge, 0.0, far)
            full = jnp.concatenate([own, pltpu.roll(own, 64, 1), near, far], axis=0)
            ext[level] = full
            high = jnp.where(group == q, pltpu.roll(full, (q * 8 - 56) % 128, 1), high)
            low = jnp.where(group == q, pltpu.roll(full, q * 8, 1), low)
        send_a[g] = jnp.where(even, high, low)
        send_b[g] = jnp.where(even, low, high)


def band_steps_kernel(ext, recv_a, recv_b, trace, one, two, coef):
    low_edge, high_edge = y_edges()
    even = lax.rem(lax.axis_index("gy"), 2) == 0
    lane = lanes((32, 128))
    for g in range(3):
        a, b = recv_a[g], recv_b[g]
        high = jnp.where(high_edge, 0.0, jnp.where(even, a, b))
        low = jnp.where(low_edge, 0.0, jnp.where(even, b, a))
        for q in range(16):
            level = g * 16 + q
            if level > 46:
                continue
            full = jnp.where(
                lane < 64,
                ext[level],
                jnp.where(
                    lane < 72,
                    pltpu.roll(high, (64 - q * 8) % 128, 1),
                    jnp.where(lane >= 120, pltpu.roll(low, (120 - q * 8) % 128, 1), 0.0),
                ),
            )
            if level < 17:
                one[level] = full
            elif level < 32:
                two[level - 16] = full
            else:
                coef[level - 31] = full
    first = lanes((8, 128)) < 64
    now, old = one, two
    for step in range(1, STEPS + 1):
        for j in range(step, 17 - step):
            u = now[j]
            beside = pltpu.roll(u, 1, 0) + pltpu.roll(u, 31, 0) + pltpu.roll(u, 1, 1) + pltpu.roll(u, 127, 1)
            lap = beside + now[j - 1] + now[j + 1] - 6.0 * u
            old[j] = 2.0 * u - old[j] + coef[j] * lap
        now, old = old, now
        plane = now[8]
        trace[:, step - 1, :] = jnp.where(first, plane[0:8], pltpu.roll(plane[8:16], 64, 1))


def pick_kernel(table, index, out):
    me = lax.axis_index("gy")
    count = table.shape[0]

    def tile(t):
        cell = jnp.broadcast_to(index[pl.ds(t, 1), :], (8, 128))
        x, y = cell >> 8, cell & 255
        place = ((x >> 4) << 3) + (x & 7)
        place = jnp.where((y >> 6) == me, place, -1)
        lane = (((x >> 3) & 1) << 6) + (y & 63)
        accs = [jnp.zeros((8, 128), F32) for _ in range(4)]
        for k in range(count):
            found = jnp.take_along_axis(table[k], lane, axis=1)
            accs[k % 4] = jnp.where(place == k, found, accs[k % 4])
        out[t] = (accs[0] + accs[1]) + (accs[2] + accs[3])

    def tiles(i, carry):
        for t in range(2):
            tile(i * 2 + t)
        return carry

    lax.fori_loop(0, index.shape[0] // 2, tiles, 0)


def spring_values(cls, k, count, modulus, yields):
    mod = jnp.zeros(cls.shape, F32)
    lim = jnp.zeros(cls.shape, F32)
    for c in range(8):
        hit = cls == c
        mod = jnp.where(hit, modulus[c, k], mod)
        lim = jnp.where(hit, jnp.where(k < count[c], yields[c, k], 0.0), lim)
    return mod, lim


def columns_kernel(count, modulus, yields, soil, start, out, edge, mods, lims, springs):
    width = soil.shape[1]

    def rows(r, carry):
        at = pl.ds(pl.multiple_of(r * 8, 8), 8)
        cls = soil[at, :]
        for k in range(16):
            mod, lim = spring_values(cls, k, count, modulus, yields)
            mods[k, at, :] = mod
            lims[k, at, :] = lim
            springs[k, at, :] = jnp.zeros((8, width), F32)
        return carry

    lax.fori_loop(0, 8, rows, 0)
    row = lax.broadcasted_iota(jnp.int32, (64, width), 0)

    def step(s, state):
        disp, vel, old = state
        strain = pltpu.roll(disp, 63, 0) - disp
        inc = strain - old
        parts = []
        for r in range(0, 64, 16):
            here = slice(r, r + 16)
            change = inc[here]
            stress = jnp.zeros((16, width), F32)
            for k in range(16):
                lim = lims[k, here, :]
                value = jnp.minimum(jnp.maximum(springs[k, here, :] + mods[k, here, :] * change, -lim), lim)
                springs[k, here, :] = value
                stress = stress + value
            parts.append(stress)
        stress = jnp.concatenate(parts, axis=0)
        edge[pl.ds(s, 1), :] = stress[55:56]
        above = jnp.where(row == 0, 0.0, pltpu.roll(stress, 1, 0))
        vel = vel + stress_rate * (stress - above)
        return disp + vel, vel, strain

    zero = jnp.zeros((64, width), F32)
    out[...] = lax.fori_loop(0, STEPS, step, (start[...], zero, zero))[0]


def last_rows_kernel(count, modulus, yields, soil, start, edge, arrived, done, out):
    del done
    row = lax.broadcasted_iota(jnp.int32, (8, 128), 0)
    for t in range(4):
        cols = slice(t * 128, (t + 1) * 128)
        base = arrived[0, t * 8 : t * 8 + 8]
        for source in range(1, arrived.shape[0]):
            base = base + arrived[source, t * 8 : t * 8 + 8]
        cls = soil[:, cols]
        pairs = [spring_values(cls, k, count, modulus, yields) for k in range(16)]
        springs = [jnp.zeros((8, 128), F32) for _ in range(16)]
        disp = start[:, cols]
        vel = jnp.zeros((8, 128), F32)
        old = jnp.zeros((8, 128), F32)
        for s in range(STEPS):
            strain = jnp.where(row == 7, base[s : s + 1], pltpu.roll(disp, 7, 0)) - disp
            inc = strain - old
            old = strain
            for k in range(16):
                mod, lim = pairs[k]
                springs[k] = jnp.minimum(jnp.maximum(springs[k] + mod * inc, -lim), lim)
            sums = springs
            while len(sums) > 1:
                sums = [sums[i] + sums[i + 1] for i in range(0, len(sums), 2)]
            stress = sums[0]
            above = jnp.where(row == 0, edge[s : s + 1, cols], pltpu.roll(stress, 1, 0))
            vel = vel + stress_rate * (stress - above)
            disp = disp + vel
        out[:, cols] = disp


RIGHT = ((8, 8, 0), (9, 7, 8), (9, 7, 15))
LEFT = ((0, 8, 0), (0, 7, 8), (0, 7, 15))


def start_jobs(jobs, sems):
    copies = [(cond, pltpu.make_async_copy(src, dst, sems.at[n])) for n, (cond, src, dst) in enumerate(jobs)]
    for cond, copy in copies:
        if cond is None:
            copy.start()
        else:
            pl.when(cond)(copy.start)
    return copies


def wait_jobs(copies):
    for cond, copy in copies:
        if cond is None:
            copy.wait()
        else:
            pl.when(cond)(copy.wait)


def run_jobs(jobs, sems):
    wait_jobs(start_jobs(jobs, sems))


def pack_x_kernel(u, p, c, edge_right, edge_left, mid_right, mid_left, mid_far, sems):
    jobs = []
    gx = lax.axis_index("gx")
    for plan, edge, mid, ends in (
        (RIGHT, edge_right, mid_right, gx == lax.axis_size("gx") - 1),
        (LEFT, edge_left, mid_left, gx == 0),
    ):
        for ref, (x0, n, at) in zip((u, p, c), plan):
            middle = ref.at[x0 : x0 + n, 8:56, :]
            jobs.append((None, ref.at[x0 : x0 + n, 0:8, :], edge.at[at : at + n, 0:8, :]))
            jobs.append((None, ref.at[x0 : x0 + n, 56:64, :], edge.at[at : at + n, 8:16, :]))
            jobs.append((None, middle, mid.at[at : at + n, :, :]))
            jobs.append((ends, middle, mid_far.at[at : at + n, :, :]))
    run_jobs(jobs, sems)


def pack_y_kernel(u, p, c, from_left, from_right, send_a, send_b, sems):
    odd = lax.rem(lax.axis_index("gy"), 2)
    pairs = []
    for send, side in ((send_a, 1 - odd), (send_b, odd)):
        own = pl.ds(pl.multiple_of(side * 56, 8), 8)
        corner = pl.ds(pl.multiple_of(side * 8, 8), 8)
        for n, ref in enumerate((u, p, c)):
            pairs.append((None, ref.at[:, own, :], send.at[16 * n : 16 * n + 16]))
        pairs.append((None, from_left.at[:, corner, :], send.at[48:70]))
        pairs.append((None, from_right.at[:, corner, :], send.at[70:92]))
    run_jobs(pairs, sems)


def region_kernel(u, p, c, el, er, ml, mr, relayed, ya, yb, out, one, two, coef, sems):
    low_x, high_x = x_edges()
    low_y, high_y = y_edges()
    even = lax.rem(lax.axis_index("gy"), 2) == 0
    bufs = (one, two, coef)
    gx = lax.axis_index("gx")
    first, final = gx == 0, gx == lax.axis_size("gx") - 1
    jobs = []

    def job(cond, src, dst):
        jobs.append((cond, src, dst))

    for ref, buf in zip((u, p, c), bufs):
        job(None, ref, buf.at[0:16, 16:80, :])
    left_at = ((24, 8, 0), (25, 7, 8), (25, 7, 15))
    right_at = ((16, 8, 0), (16, 7, 8), (16, 7, 15))
    for cond, far, plan, edge, mid in ((~low_x, first, left_at, el, ml), (~high_x, final, right_at, er, mr)):
        for buf, (x0, n, at) in zip(bufs, plan):
            job(~far, mid.at[at : at + n], buf.at[x0 : x0 + n, 24:72, :])
            job(far & cond, relayed.at[at : at + n], buf.at[x0 : x0 + n, 24:72, :])
            job(cond, edge.at[at : at + n, 0:8, :], buf.at[x0 : x0 + n, 16:24, :])
            job(cond, edge.at[at : at + n, 8:16, :], buf.at[x0 : x0 + n, 72:80, :])
    for msg, is_high in ((ya, even), (yb, ~even)):
        for rows, cond in (((80, 88), is_high & ~high_y), ((8, 16), ~is_high & ~low_y)):
            for n, buf in enumerate(bufs):
                job(cond, msg.at[16 * n : 16 * n + 16], buf.at[0:16, rows[0] : rows[1], :])
            for more, plan, base in ((~low_x, left_at, 48), (~high_x, right_at, 70)):
                for buf, (x0, n, at) in zip(bufs, plan):
                    job(
                        cond & more,
                        msg.at[base + at : base + at + n],
                        buf.at[x0 : x0 + n, rows[0] : rows[1], :],
                    )
    copies = start_jobs(jobs, sems)
    for edge, x0, n, y0, m in (
        (low_x, 24, 8, 8, 80),
        (high_x, 16, 8, 8, 80),
        (low_y, 0, 32, 8, 8),
        (high_y, 0, 32, 80, 8),
    ):

        @pl.when(edge)
        def _():
            for buf in bufs:
                buf[x0 : x0 + n, y0 : y0 + m, :] = jnp.zeros((n, m, 256), F32)

    wait_jobs(copies)

    now, old = one, two
    halves = (slice(0, 128), slice(128, 256))
    rows = 16
    lane = lanes((rows, 128))
    top, end = lane == 0, lane == 127
    for step in range(1, STEPS + 1):
        last = step == STEPS
        for x in range(step - HALO, 16 + HALO - step):
            at, lower, upper = x % 32, (x - 1) % 32, (x + 1) % 32
            for y0 in range(16, 80, rows) if last else range(8, 88, rows):
                here = slice(y0, y0 + rows)
                a, b = (now[at, here, h] for h in halves)
                ra, rb = pltpu.roll(a, 1, 1), pltpu.roll(b, 1, 1)
                la, lb = pltpu.roll(a, 127, 1), pltpu.roll(b, 127, 1)
                depth = (
                    jnp.where(top, a, ra) + jnp.where(end, lb, la),
                    jnp.where(top, ra, rb) + jnp.where(end, 0.0, lb),
                )
                for h, v, dz in zip(halves, (a, b), depth):
                    beside = now[lower, here, h] + now[upper, here, h]
                    beside = beside + (now[at, y0 - 1 : y0 - 1 + rows, h] + now[at, y0 + 1 : y0 + 1 + rows, h])
                    lap = beside + dz - 6.0 * v
                    value = (2.0 * v - old[at, here, h]) + coef[at, here, h] * lap
                    if last:
                        out[x, y0 - 16 : y0 - 16 + rows, h] = value
                    else:
                        old[at, here, h] = value
        now, old = old, now


def relays(n_sec, n_gx):
    def at(sec, gx, gy):
        return (sec % n_sec * n_gx + gx) * 4 + gy

    top = n_gx - 1
    out, into = [], []
    for sec in range(n_sec):
        for gy in range(4):
            up, down = ((3, 12), (11, 4))[gy % 2]
            out += [(at(sec, top, gy), at(sec, up, gy)), (at(sec, 0, gy), at(sec, down, gy))]
            if sec < n_sec - 1:
                into.append((at(sec, up, gy), at(sec + 1, 0, gy)))
            if sec > 0:
                into.append((at(sec, down, gy), at(sec - 1, top, gy)))
    return out, into


def shards(
    reg_disp,
    reg_prev,
    reg_coef,
    basin_disp,
    face_index,
    soil_class,
    spring_count,
    spring_modulus,
    spring_yield,
):
    n_gx = lax.axis_size("gx")
    n_x = lax.axis_size("sec") * n_gx
    right = [(i, (i + 1) % n_x) for i in range(n_x)]
    left = [(i, (i - 1) % n_x) for i in range(n_x)]
    swap_a = [(0, 1), (1, 0), (2, 3), (3, 2)]
    swap_b = [(0, 0), (1, 2), (2, 1), (3, 3)]
    regional = (reg_disp, reg_prev, reg_coef)
    half = pl.BlockSpec((16, 64, 128), lambda i: (0, 0, 0))
    whole = lambda *s: pl.BlockSpec(s, lambda i: (0,) * len(s))
    band, band_right, band_left = pl.pallas_call(
        band_kernel,
        grid=(1,),
        out_shape=(sds(48, 8, 128), sds(24, 8, 128), sds(24, 8, 128)),
        in_specs=[half] * 3,
        out_specs=(whole(48, 8, 128), whole(24, 8, 128), whole(24, 8, 128)),
        compiler_params=LARGE,
        name="band",
    )(*regional)
    band_from_left = lax.ppermute(band_right, XAX, right)
    band_from_right = lax.ppermute(band_left, XAX, left)
    index, _ = lax.optimization_barrier((face_index.reshape(1, 4, 128), band_right))
    index = lax.all_gather(index, "gy").reshape(16, 128)

    regional, index = lax.optimization_barrier((regional, index))
    edge_right, edge_left, mid_right, mid_left, mid_far = pl.pallas_call(
        pack_x_kernel,
        out_shape=(sds(22, 16, 256), sds(22, 16, 256), sds(22, 48, 256), sds(22, 48, 256), sds(22, 48, 256)),
        in_specs=[ANY] * 3,
        out_specs=(ANY,) * 5,
        scratch_shapes=[pltpu.SemaphoreType.DMA((24,))],
        compiler_params=PARAMS,
        name="pack_x",
    )(*regional)
    edge_from_left = lax.ppermute(edge_right, XAX, right)
    edge_from_right = lax.ppermute(edge_left, XAX, left)
    mid_from_left = lax.ppermute(mid_right, "gx", [(i, i + 1) for i in range(n_gx - 1)])
    mid_from_right = lax.ppermute(mid_left, "gx", [(i + 1, i) for i in range(n_gx - 1)])

    soil = soil_class[0]
    start = basin_disp[0]
    soil, start, _ = lax.optimization_barrier((soil, start, index))
    tables = (spring_count, spring_modulus, spring_yield)
    block = pl.BlockSpec((64, 256), lambda i: (0, i))
    upper, edge = pl.pallas_call(
        columns_kernel,
        grid=(2,),
        out_shape=(sds(64, 512), sds(8, 512)),
        in_specs=[SM] * 3 + [block] * 2,
        out_specs=(block, pl.BlockSpec((8, 256), lambda i: (0, i))),
        scratch_shapes=[pltpu.VMEM((16, 64, 256), F32)] * 3,
        compiler_params=PARAMS,
        name="columns",
    )(*tables, soil, start)

    upper, band_from_left, band_from_right = lax.optimization_barrier((upper, band_from_left, band_from_right))
    relay_out, relay_in = relays(lax.axis_size("sec"), n_gx)
    mid_far, band_from_left, band_from_right = lax.optimization_barrier((mid_far, band_from_left, band_from_right))
    mid_relay = lax.ppermute(mid_far, ALL, relay_out)
    mid_relay = lax.ppermute(mid_relay, ALL, relay_in)

    ext, band_a, band_b = pl.pallas_call(
        band_edges_kernel,
        out_shape=(sds(48, 32, 128), sds(3, 32, 128), sds(3, 32, 128)),
        in_specs=[VM] * 3,
        out_specs=(VM,) * 3,
        compiler_params=PARAMS,
        name="band_edges",
    )(band, band_from_left, band_from_right)
    band_a = lax.ppermute(band_a, "gy", swap_a)
    band_b = lax.ppermute(band_b, "gy", swap_b)
    trace = pl.pallas_call(
        band_steps_kernel,
        out_shape=sds(8, 8, 128),
        in_specs=[VM] * 3,
        out_specs=VM,
        scratch_shapes=[pltpu.VMEM((17, 32, 128), F32)] * 3,
        compiler_params=PARAMS,
        name="band_steps",
    )(ext, band_a, band_b)

    table = lax.all_to_all(jnp.broadcast_to(trace.reshape(1, 64, 128), (n_gx, 64, 128)), "gx", 0, 0)
    table = table.reshape(n_gx * 8, 8, 128)
    table, edge_from_left, edge_from_right = lax.optimization_barrier((table, edge_from_left, edge_from_right))
    y_a, y_b = pl.pallas_call(
        pack_y_kernel,
        out_shape=(sds(92, 8, 256), sds(92, 8, 256)),
        in_specs=[ANY] * 5,
        out_specs=(ANY,) * 2,
        scratch_shapes=[pltpu.SemaphoreType.DMA((10,))],
        compiler_params=PARAMS,
        name="pack_y",
    )(*regional, edge_from_left, edge_from_right)
    table, y_a, y_b = lax.optimization_barrier((table, y_a, y_b))
    y_a = lax.ppermute(y_a, "gy", swap_a)
    y_b = lax.ppermute(y_b, "gy", swap_b)

    picked = pl.pallas_call(
        pick_kernel,
        out_shape=sds(16, 8, 128),
        in_specs=[VM] * 2,
        out_specs=VM,
        compiler_params=PARAMS,
        name="pick",
    )(table, index)
    arrived = lax.all_to_all(picked.reshape(4, 32, 128), "gy", 0, 0)

    tail = pl.BlockSpec((8, 512), lambda i: (7, 0))
    basin = pl.pallas_call(
        last_rows_kernel,
        grid=(1,),
        out_shape=sds(64, 512),
        in_specs=[SM] * 3 + [tail, tail, whole(8, 512), whole(4, 32, 128), ANY],
        out_specs=tail,
        input_output_aliases={7: 0},
        compiler_params=PARAMS,
        name="last_rows",
    )(*tables, soil, start, edge, arrived, upper)

    final = pl.pallas_call(
        region_kernel,
        out_shape=sds(16, 64, 256),
        in_specs=[ANY] * 10,
        out_specs=VM,
        scratch_shapes=[pltpu.VMEM((32, 96, 256), F32)] * 3 + [pltpu.SemaphoreType.DMA((64,))],
        compiler_params=PARAMS,
        name="region",
    )(*regional, edge_from_left, edge_from_right, mid_from_left, mid_from_right, mid_relay, y_a, y_b)
    return (final, basin[None])


def solution(mesh):
    in_specs = (
        P(("sec", "gx"), "gy", None),
        P(("sec", "gx"), "gy", None),
        P(("sec", "gx"), "gy", None),
        P("sec", None, ("gx", "gy")),
        P("sec", ("gx", "gy")),
        P("sec", None, ("gx", "gy")),
        P(),
        P(),
        P(),
    )
    out_specs = (P(("sec", "gx"), "gy", None), P("sec", None, ("gx", "gy")))
    return jax.shard_map(shards, mesh=mesh, in_specs=in_specs, out_specs=out_specs, check_vma=False)
```

```python
import functools
import jax
import jax.numpy as jnp
from jax import lax
from jax.experimental import pallas as pl
from jax.experimental.pallas import tpu as pltpu
from jax.sharding import PartitionSpec as P

STEPS = 8
HALO = 8
FDEP = 64
stress_rate = 0.5
XAX = ("sec", "gx")
ALL = ("sec", "gx", "gy")
F32 = jnp.float32
ANY = pl.BlockSpec(memory_space=pl.ANY)
VM = pl.BlockSpec(memory_space=pltpu.VMEM)
SM = pl.BlockSpec(memory_space=pltpu.SMEM)
PARAMS = pltpu.CompilerParams(vmem_limit_bytes=40 * 1024 * 1024)
LARGE = pltpu.CompilerParams(vmem_limit_bytes=60 * 1024 * 1024)


def sds(*shape):
    return jax.ShapeDtypeStruct(shape, F32)


def x_edges():
    at = lax.axis_index("sec") * lax.axis_size("gx") + lax.axis_index("gx")
    return at == 0, at == lax.axis_size("sec") * lax.axis_size("gx") - 1


def y_edges():
    at = lax.axis_index("gy")
    return at == 0, at == lax.axis_size("gy") - 1


def lanes(shape):
    return lax.broadcasted_iota(jnp.int32, shape, len(shape) - 1)


def band_kernel(u, p, c, band, to_right, to_left):
    lane = lanes((64, 128))
    for x in range(8):
        halves = []
        for row in (x, x + 8):
            halves.append(
                jnp.where(
                    lane < 73,
                    u[row],
                    jnp.where(lane < 88, pltpu.roll(p[row], 16, 1), pltpu.roll(c[row], 31, 1)),
                )
            )
        turned = jnp.concatenate(halves, axis=0).T
        band[:, x, :] = turned[56:104]
    first = lanes((8, 128)) < 64
    for k in range(24):
        a, b = band[k], band[k + 24]
        ra, rb = pltpu.roll(a, 64, 1), pltpu.roll(b, 64, 1)
        to_right[k] = jnp.where(first, ra, b)
        to_left[k] = jnp.where(first, a, rb)


def band_edges_kernel(band, from_left, from_right, ext, send_a, send_b):
    low_edge, high_edge = x_edges()
    even = lax.rem(lax.axis_index("gy"), 2) == 0
    lane = lanes((8, 128))
    first = lane < 64
    group = lanes((32, 128)) // 8
    for g in range(3):
        high = jnp.zeros((32, 128), F32)
        low = jnp.zeros((32, 128), F32)
        for q in range(16):
            level = g * 16 + q
            own = band[level]
            near = from_right[level % 24]
            far = from_left[level % 24]
            if level >= 24:
                near, far = pltpu.roll(near, 64, 1), pltpu.roll(far, 64, 1)
            near = jnp.where(high_edge, 0.0, near)
            far = jnp.where(low_edge, 0.0, far)
            full = jnp.concatenate([own, pltpu.roll(own, 64, 1), near, far], axis=0)
            ext[level] = full
            high = jnp.where(group == q, pltpu.roll(full, (q * 8 - 56) % 128, 1), high)
            low = jnp.where(group == q, pltpu.roll(full, q * 8, 1), low)
        send_a[g] = jnp.where(even, high, low)
        send_b[g] = jnp.where(even, low, high)


def band_steps_kernel(ext, recv_a, recv_b, trace, one, two, coef):
    low_edge, high_edge = y_edges()
    even = lax.rem(lax.axis_index("gy"), 2) == 0
    lane = lanes((32, 128))
    for g in range(3):
        a, b = recv_a[g], recv_b[g]
        high = jnp.where(high_edge, 0.0, jnp.where(even, a, b))
        low = jnp.where(low_edge, 0.0, jnp.where(even, b, a))
        for q in range(16):
            level = g * 16 + q
            if level > 46:
                continue
            full = jnp.where(
                lane < 64,
                ext[level],
                jnp.where(
                    lane < 72,
                    pltpu.roll(high, (64 - q * 8) % 128, 1),
                    jnp.where(lane >= 120, pltpu.roll(low, (120 - q * 8) % 128, 1), 0.0),
                ),
            )
            if level < 17:
                one[level] = full
            elif level < 32:
                two[level - 16] = full
            else:
                coef[level - 31] = full
    first = lanes((8, 128)) < 64
    now, old = one, two
    for step in range(1, STEPS + 1):
        for j in range(step, 17 - step):
            u = now[j]
            beside = pltpu.roll(u, 1, 0) + pltpu.roll(u, 31, 0) + pltpu.roll(u, 1, 1) + pltpu.roll(u, 127, 1)
            lap = beside + now[j - 1] + now[j + 1] - 6.0 * u
            old[j] = 2.0 * u - old[j] + coef[j] * lap
        now, old = old, now
        plane = now[8]
        trace[:, step - 1, :] = jnp.where(first, plane[0:8], pltpu.roll(plane[8:16], 64, 1))


def pick_kernel(table, index, *outs):
    me = lax.axis_index("gy")
    count = table.shape[0]

    def tile(row):
        cell = jnp.broadcast_to(index[pl.ds(row, 1), :], (8, 128))
        x, y = cell >> 8, cell & 255
        place = ((x >> 4) << 3) + (x & 7)
        place = jnp.where((y >> 6) == me, place, -1)
        lane = (((x >> 3) & 1) << 6) + (y & 63)
        accs = [jnp.zeros((8, 128), F32) for _ in range(4)]
        for k in range(count):
            found = jnp.take_along_axis(table[k], lane, axis=1)
            accs[k % 4] = jnp.where(place == k, found, accs[k % 4])
        return (accs[0] + accs[1]) + (accs[2] + accs[3])

    def tiles(t, carry):
        for j, out in enumerate(outs):
            out[t] = tile(lax.rem(me + j, 4) * 4 + t)
        return carry

    lax.fori_loop(0, 4, tiles, 0)


def spring_values(cls, k, count, modulus, yields):
    mod = jnp.zeros(cls.shape, F32)
    lim = jnp.zeros(cls.shape, F32)
    for c in range(8):
        hit = cls == c
        mod = jnp.where(hit, modulus[c, k], mod)
        lim = jnp.where(hit, jnp.where(k < count[c], yields[c, k], 0.0), lim)
    return mod, lim


def columns_kernel(count, modulus, yields, soil, start, out, edge, mods, lims, springs):
    width = soil.shape[1]

    def rows(r, carry):
        at = pl.ds(pl.multiple_of(r * 8, 8), 8)
        cls = soil[at, :]
        for k in range(16):
            mod, lim = spring_values(cls, k, count, modulus, yields)
            mods[k, at, :] = mod
            lims[k, at, :] = lim
            springs[k, at, :] = jnp.zeros((8, width), F32)
        return carry

    lax.fori_loop(0, 8, rows, 0)
    row = lax.broadcasted_iota(jnp.int32, (64, width), 0)

    def step(s, state):
        disp, vel, old = state
        strain = pltpu.roll(disp, 63, 0) - disp
        inc = strain - old
        parts = []
        for r in range(0, 64, 16):
            here = slice(r, r + 16)
            change = inc[here]
            stress = jnp.zeros((16, width), F32)
            for k in range(16):
                lim = lims[k, here, :]
                value = jnp.minimum(jnp.maximum(springs[k, here, :] + mods[k, here, :] * change, -lim), lim)
                springs[k, here, :] = value
                stress = stress + value
            parts.append(stress)
        stress = jnp.concatenate(parts, axis=0)
        edge[pl.ds(s, 1), :] = stress[55:56]
        above = jnp.where(row == 0, 0.0, pltpu.roll(stress, 1, 0))
        vel = vel + stress_rate * (stress - above)
        return disp + vel, vel, strain

    zero = jnp.zeros((64, width), F32)
    out[...] = lax.fori_loop(0, STEPS, step, (start[...], zero, zero))[0]


def last_rows_kernel(count, modulus, yields, soil, start, edge, own, next1, next2, next3, done, out):
    del done
    row = lax.broadcasted_iota(jnp.int32, (8, 128), 0)
    for t in range(4):
        cols = slice(t * 128, (t + 1) * 128)
        base = (own[t] + next1[t]) + (next2[t] + next3[t])
        cls = soil[:, cols]
        pairs = [spring_values(cls, k, count, modulus, yields) for k in range(16)]
        springs = [jnp.zeros((8, 128), F32) for _ in range(16)]
        disp = start[:, cols]
        vel = jnp.zeros((8, 128), F32)
        old = jnp.zeros((8, 128), F32)
        for s in range(STEPS):
            strain = jnp.where(row == 7, base[s : s + 1], pltpu.roll(disp, 7, 0)) - disp
            inc = strain - old
            old = strain
            for k in range(16):
                mod, lim = pairs[k]
                springs[k] = jnp.minimum(jnp.maximum(springs[k] + mod * inc, -lim), lim)
            sums = springs
            while len(sums) > 1:
                sums = [sums[i] + sums[i + 1] for i in range(0, len(sums), 2)]
            stress = sums[0]
            above = jnp.where(row == 0, edge[s : s + 1, cols], pltpu.roll(stress, 1, 0))
            vel = vel + stress_rate * (stress - above)
            disp = disp + vel
        out[:, cols] = disp


RIGHT = ((8, 8, 0), (9, 7, 8), (9, 7, 15))
LEFT = ((0, 8, 0), (0, 7, 8), (0, 7, 15))


def start_jobs(jobs, sems):
    copies = [(cond, pltpu.make_async_copy(src, dst, sems.at[n])) for n, (cond, src, dst) in enumerate(jobs)]
    for cond, copy in copies:
        if cond is None:
            copy.start()
        else:
            pl.when(cond)(copy.start)
    return copies


def wait_jobs(copies):
    for cond, copy in copies:
        if cond is None:
            copy.wait()
        else:
            pl.when(cond)(copy.wait)


def run_jobs(jobs, sems):
    wait_jobs(start_jobs(jobs, sems))


def pack_x_kernel(u, p, c, edge_right, edge_left, mid_right, mid_left, mid_far, sems):
    jobs = []
    gx = lax.axis_index("gx")
    for plan, edge, mid, ends in (
        (RIGHT, edge_right, mid_right, gx == lax.axis_size("gx") - 1),
        (LEFT, edge_left, mid_left, gx == 0),
    ):
        for ref, (x0, n, at) in zip((u, p, c), plan):
            middle = ref.at[x0 : x0 + n, 8:56, :]
            jobs.append((None, ref.at[x0 : x0 + n, 0:8, :], edge.at[at : at + n, 0:8, :]))
            jobs.append((None, ref.at[x0 : x0 + n, 56:64, :], edge.at[at : at + n, 8:16, :]))
            jobs.append((None, middle, mid.at[at : at + n, :, :]))
            jobs.append((ends, middle, mid_far.at[at : at + n, :, :]))
    run_jobs(jobs, sems)


def pack_y_kernel(u, p, c, from_left, from_right, send_a, send_b, sems):
    odd = lax.rem(lax.axis_index("gy"), 2)
    pairs = []
    for send, side in ((send_a, 1 - odd), (send_b, odd)):
        own = pl.ds(pl.multiple_of(side * 56, 8), 8)
        corner = pl.ds(pl.multiple_of(side * 8, 8), 8)
        for n, ref in enumerate((u, p, c)):
            pairs.append((None, ref.at[:, own, :], send.at[16 * n : 16 * n + 16]))
        pairs.append((None, from_left.at[:, corner, :], send.at[48:70]))
        pairs.append((None, from_right.at[:, corner, :], send.at[70:92]))
    run_jobs(pairs, sems)


def region_kernel(u, p, c, el, er, ml, mr, relayed, ya, yb, out, one, two, coef, sems):
    low_x, high_x = x_edges()
    low_y, high_y = y_edges()
    even = lax.rem(lax.axis_index("gy"), 2) == 0
    bufs = (one, two, coef)
    gx = lax.axis_index("gx")
    first, final = gx == 0, gx == lax.axis_size("gx") - 1
    jobs = []

    def job(cond, src, dst):
        jobs.append((cond, src, dst))

    for ref, buf in zip((u, p, c), bufs):
        job(None, ref, buf.at[0:16, 16:80, :])
    left_at = ((24, 8, 0), (25, 7, 8), (25, 7, 15))
    right_at = ((16, 8, 0), (16, 7, 8), (16, 7, 15))
    for cond, far, plan, edge, mid in ((~low_x, first, left_at, el, ml), (~high_x, final, right_at, er, mr)):
        for buf, (x0, n, at) in zip(bufs, plan):
            job(~far, mid.at[at : at + n], buf.at[x0 : x0 + n, 24:72, :])
            job(far & cond, relayed.at[at : at + n], buf.at[x0 : x0 + n, 24:72, :])
            job(cond, edge.at[at : at + n, 0:8, :], buf.at[x0 : x0 + n, 16:24, :])
            job(cond, edge.at[at : at + n, 8:16, :], buf.at[x0 : x0 + n, 72:80, :])
    for msg, is_high in ((ya, even), (yb, ~even)):
        for rows, cond in (((80, 88), is_high & ~high_y), ((8, 16), ~is_high & ~low_y)):
            for n, buf in enumerate(bufs):
                job(cond, msg.at[16 * n : 16 * n + 16], buf.at[0:16, rows[0] : rows[1], :])
            for more, plan, base in ((~low_x, left_at, 48), (~high_x, right_at, 70)):
                for buf, (x0, n, at) in zip(bufs, plan):
                    job(
                        cond & more,
                        msg.at[base + at : base + at + n],
                        buf.at[x0 : x0 + n, rows[0] : rows[1], :],
                    )
    copies = start_jobs(jobs, sems)
    for edge, x0, n, y0, m in (
        (low_x, 24, 8, 8, 80),
        (high_x, 16, 8, 8, 80),
        (low_y, 0, 32, 8, 8),
        (high_y, 0, 32, 80, 8),
    ):

        @pl.when(edge)
        def _():
            for buf in bufs:
                buf[x0 : x0 + n, y0 : y0 + m, :] = jnp.zeros((n, m, 256), F32)

    wait_jobs(copies)

    now, old = one, two
    halves = (slice(0, 128), slice(128, 256))
    rows = 16
    lane = lanes((rows, 128))
    top, end = lane == 0, lane == 127
    for step in range(1, STEPS + 1):
        last = step == STEPS
        for x in range(step - HALO, 16 + HALO - step):
            at, lower, upper = x % 32, (x - 1) % 32, (x + 1) % 32
            for y0 in range(16, 80, rows) if last else range(8, 88, rows):
                here = slice(y0, y0 + rows)
                a, b = (now[at, here, h] for h in halves)
                ra, rb = pltpu.roll(a, 1, 1), pltpu.roll(b, 1, 1)
                la, lb = pltpu.roll(a, 127, 1), pltpu.roll(b, 127, 1)
                depth = (
                    jnp.where(top, a, ra) + jnp.where(end, lb, la),
                    jnp.where(top, ra, rb) + jnp.where(end, 0.0, lb),
                )
                for h, v, dz in zip(halves, (a, b), depth):
                    beside = now[lower, here, h] + now[upper, here, h]
                    beside = beside + (now[at, y0 - 1 : y0 - 1 + rows, h] + now[at, y0 + 1 : y0 + 1 + rows, h])
                    lap = beside + dz - 6.0 * v
                    value = (2.0 * v - old[at, here, h]) + coef[at, here, h] * lap
                    if last:
                        out[x, y0 - 16 : y0 - 16 + rows, h] = value
                    else:
                        old[at, here, h] = value
        now, old = old, now


def relays(n_sec, n_gx):
    def at(sec, gx, gy):
        return (sec % n_sec * n_gx + gx) * 4 + gy

    top = n_gx - 1
    out, into = [], []
    for sec in range(n_sec):
        for gy in range(4):
            up, down = ((3, 12), (11, 4))[gy % 2]
            out += [(at(sec, top, gy), at(sec, up, gy)), (at(sec, 0, gy), at(sec, down, gy))]
            if sec < n_sec - 1:
                into.append((at(sec, up, gy), at(sec + 1, 0, gy)))
            if sec > 0:
                into.append((at(sec, down, gy), at(sec - 1, top, gy)))
    return out, into


def shards(
    reg_disp,
    reg_prev,
    reg_coef,
    basin_disp,
    face_index,
    soil_class,
    spring_count,
    spring_modulus,
    spring_yield,
):
    n_gx = lax.axis_size("gx")
    n_x = lax.axis_size("sec") * n_gx
    right = [(i, (i + 1) % n_x) for i in range(n_x)]
    left = [(i, (i - 1) % n_x) for i in range(n_x)]
    swap_a = [(0, 1), (1, 0), (2, 3), (3, 2)]
    swap_b = [(0, 0), (1, 2), (2, 1), (3, 3)]
    regional = (reg_disp, reg_prev, reg_coef)
    half = pl.BlockSpec((16, 64, 128), lambda i: (0, 0, 0))
    whole = lambda *s: pl.BlockSpec(s, lambda i: (0,) * len(s))
    band, band_right, band_left = pl.pallas_call(
        band_kernel,
        grid=(1,),
        out_shape=(sds(48, 8, 128), sds(24, 8, 128), sds(24, 8, 128)),
        in_specs=[half] * 3,
        out_specs=(whole(48, 8, 128), whole(24, 8, 128), whole(24, 8, 128)),
        compiler_params=LARGE,
        name="band",
    )(*regional)
    band_from_left = lax.ppermute(band_right, XAX, right)
    band_from_right = lax.ppermute(band_left, XAX, left)
    index, _ = lax.optimization_barrier((face_index.reshape(1, 4, 128), band_right))
    index = lax.all_gather(index, "gy").reshape(16, 128)

    regional, index = lax.optimization_barrier((regional, index))
    edge_right, edge_left, mid_right, mid_left, mid_far = pl.pallas_call(
        pack_x_kernel,
        out_shape=(sds(22, 16, 256), sds(22, 16, 256), sds(22, 48, 256), sds(22, 48, 256), sds(22, 48, 256)),
        in_specs=[ANY] * 3,
        out_specs=(ANY,) * 5,
        scratch_shapes=[pltpu.SemaphoreType.DMA((24,))],
        compiler_params=PARAMS,
        name="pack_x",
    )(*regional)
    edge_from_left = lax.ppermute(edge_right, XAX, right)
    edge_from_right = lax.ppermute(edge_left, XAX, left)

    soil = soil_class[0]
    start = basin_disp[0]
    soil, start, _ = lax.optimization_barrier((soil, start, index))
    tables = (spring_count, spring_modulus, spring_yield)
    block = pl.BlockSpec((64, 256), lambda i: (0, i))
    upper, edge = pl.pallas_call(
        columns_kernel,
        grid=(2,),
        out_shape=(sds(64, 512), sds(8, 512)),
        in_specs=[SM] * 3 + [block] * 2,
        out_specs=(block, pl.BlockSpec((8, 256), lambda i: (0, i))),
        scratch_shapes=[pltpu.VMEM((16, 64, 256), F32)] * 3,
        compiler_params=PARAMS,
        name="columns",
    )(*tables, soil, start)

    upper, band_from_left, band_from_right = lax.optimization_barrier((upper, band_from_left, band_from_right))
    relay_out, relay_in = relays(lax.axis_size("sec"), n_gx)
    mid_far, band_from_left, band_from_right = lax.optimization_barrier((mid_far, band_from_left, band_from_right))
    mid_relay = lax.ppermute(mid_far, ALL, relay_out)
    mid_relay = lax.ppermute(mid_relay, ALL, relay_in)

    ext, band_a, band_b = pl.pallas_call(
        band_edges_kernel,
        out_shape=(sds(48, 32, 128), sds(3, 32, 128), sds(3, 32, 128)),
        in_specs=[VM] * 3,
        out_specs=(VM,) * 3,
        compiler_params=PARAMS,
        name="band_edges",
    )(band, band_from_left, band_from_right)
    band_a = lax.ppermute(band_a, "gy", swap_a)
    band_b = lax.ppermute(band_b, "gy", swap_b)
    trace = pl.pallas_call(
        band_steps_kernel,
        out_shape=sds(8, 8, 128),
        in_specs=[VM] * 3,
        out_specs=VM,
        scratch_shapes=[pltpu.VMEM((17, 32, 128), F32)] * 3,
        compiler_params=PARAMS,
        name="band_steps",
    )(ext, band_a, band_b)

    table = lax.all_to_all(jnp.broadcast_to(trace.reshape(1, 64, 128), (n_gx, 64, 128)), "gx", 0, 0)
    table = table.reshape(n_gx * 8, 8, 128)
    mid_from_left = lax.ppermute(mid_right, "gx", [(i, i + 1) for i in range(n_gx - 1)])
    mid_from_right = lax.ppermute(mid_left, "gx", [(i + 1, i) for i in range(n_gx - 1)])
    trace, edge_from_left, edge_from_right = lax.optimization_barrier((trace, edge_from_left, edge_from_right))
    y_a, y_b = pl.pallas_call(
        pack_y_kernel,
        out_shape=(sds(92, 8, 256), sds(92, 8, 256)),
        in_specs=[ANY] * 5,
        out_specs=(ANY,) * 2,
        scratch_shapes=[pltpu.SemaphoreType.DMA((10,))],
        compiler_params=PARAMS,
        name="pack_y",
    )(*regional, edge_from_left, edge_from_right)
    y_a = lax.ppermute(y_a, "gy", swap_a)
    y_b = lax.ppermute(y_b, "gy", swap_b)

    picked = pl.pallas_call(
        pick_kernel,
        out_shape=(sds(4, 8, 128),) * 4,
        in_specs=[VM] * 2,
        out_specs=(VM,) * 4,
        compiler_params=PARAMS,
        name="pick",
    )(table, index)
    y_b, *picked = lax.optimization_barrier((y_b, *picked))
    arrived = [picked[0]] + [
        lax.ppermute(picked[k], "gy", [(i, (i + k) % 4) for i in range(4)]) for k in (1, 2, 3)
    ]

    final = pl.pallas_call(
        region_kernel,
        out_shape=sds(16, 64, 256),
        in_specs=[ANY] * 10,
        out_specs=VM,
        scratch_shapes=[pltpu.VMEM((32, 96, 256), F32)] * 3 + [pltpu.SemaphoreType.DMA((64,))],
        compiler_params=PARAMS,
        name="region",
    )(*regional, edge_from_left, edge_from_right, mid_from_left, mid_from_right, mid_relay, y_a, y_b)
    final, *arrived = lax.optimization_barrier((final, *arrived))
    tail = pl.BlockSpec((8, 512), lambda i: (7, 0))
    basin = pl.pallas_call(
        last_rows_kernel,
        grid=(1,),
        out_shape=sds(64, 512),
        in_specs=[SM] * 3 + [tail, tail, whole(8, 512)] + [whole(4, 8, 128)] * 4 + [ANY],
        out_specs=tail,
        input_output_aliases={10: 0},
        compiler_params=PARAMS,
        name="last_rows",
    )(*tables, soil, start, edge, *arrived, upper)
    return (final, basin[None])


def solution(mesh):
    in_specs = (
        P(("sec", "gx"), "gy", None),
        P(("sec", "gx"), "gy", None),
        P(("sec", "gx"), "gy", None),
        P("sec", None, ("gx", "gy")),
        P("sec", ("gx", "gy")),
        P("sec", None, ("gx", "gy")),
        P(),
        P(),
        P(),
    )
    out_specs = (P(("sec", "gx"), "gy", None), P("sec", None, ("gx", "gy")))
    return jax.shard_map(shards, mesh=mesh, in_specs=in_specs, out_specs=out_specs, check_vma=False)
```

```python
import functools
import jax
import jax.numpy as jnp
from jax import lax
from jax.experimental import pallas as pl
from jax.experimental.pallas import tpu as pltpu
from jax.sharding import PartitionSpec as P

STEPS = 8
HALO = 8
FDEP = 64
stress_rate = 0.5
XAX = ("sec", "gx")
ALL = ("sec", "gx", "gy")
F32 = jnp.float32
ANY = pl.BlockSpec(memory_space=pl.ANY)
VM = pl.BlockSpec(memory_space=pltpu.VMEM)
SM = pl.BlockSpec(memory_space=pltpu.SMEM)
PARAMS = pltpu.CompilerParams(vmem_limit_bytes=40 * 1024 * 1024)
LARGE = pltpu.CompilerParams(vmem_limit_bytes=60 * 1024 * 1024)


def sds(*shape):
    return jax.ShapeDtypeStruct(shape, F32)


def x_edges():
    at = lax.axis_index("sec") * lax.axis_size("gx") + lax.axis_index("gx")
    return at == 0, at == lax.axis_size("sec") * lax.axis_size("gx") - 1


def y_edges():
    at = lax.axis_index("gy")
    return at == 0, at == lax.axis_size("gy") - 1


def lanes(shape):
    return lax.broadcasted_iota(jnp.int32, shape, len(shape) - 1)


def band_kernel(u, p, c, band, to_right, to_left):
    lane = lanes((64, 128))
    for x in range(8):
        halves = []
        for row in (x, x + 8):
            halves.append(
                jnp.where(
                    lane < 73,
                    u[row],
                    jnp.where(lane < 88, pltpu.roll(p[row], 16, 1), pltpu.roll(c[row], 31, 1)),
                )
            )
        turned = jnp.concatenate(halves, axis=0).T
        band[:, x, :] = turned[56:104]
    first = lanes((8, 128)) < 64
    for k in range(24):
        a, b = band[k], band[k + 24]
        ra, rb = pltpu.roll(a, 64, 1), pltpu.roll(b, 64, 1)
        to_right[k] = jnp.where(first, ra, b)
        to_left[k] = jnp.where(first, a, rb)


def band_edges_kernel(band, from_left, from_right, ext, send_a, send_b):
    low_edge, high_edge = x_edges()
    even = lax.rem(lax.axis_index("gy"), 2) == 0
    lane = lanes((8, 128))
    first = lane < 64
    group = lanes((32, 128)) // 8
    for g in range(3):
        high = jnp.zeros((32, 128), F32)
        low = jnp.zeros((32, 128), F32)
        for q in range(16):
            level = g * 16 + q
            own = band[level]
            near = from_right[level % 24]
            far = from_left[level % 24]
            if level >= 24:
                near, far = pltpu.roll(near, 64, 1), pltpu.roll(far, 64, 1)
            near = jnp.where(high_edge, 0.0, near)
            far = jnp.where(low_edge, 0.0, far)
            full = jnp.concatenate([own, pltpu.roll(own, 64, 1), near, far], axis=0)
            ext[level] = full
            high = jnp.where(group == q, pltpu.roll(full, (q * 8 - 56) % 128, 1), high)
            low = jnp.where(group == q, pltpu.roll(full, q * 8, 1), low)
        send_a[g] = jnp.where(even, high, low)
        send_b[g] = jnp.where(even, low, high)


def band_steps_kernel(ext, recv_a, recv_b, copies, one, two, coef, trace):
    low_edge, high_edge = y_edges()
    even = lax.rem(lax.axis_index("gy"), 2) == 0
    lane = lanes((32, 128))
    for g in range(3):
        a, b = recv_a[g], recv_b[g]
        high = jnp.where(high_edge, 0.0, jnp.where(even, a, b))
        low = jnp.where(low_edge, 0.0, jnp.where(even, b, a))
        for q in range(16):
            level = g * 16 + q
            if level > 46:
                continue
            full = jnp.where(
                lane < 64,
                ext[level],
                jnp.where(
                    lane < 72,
                    pltpu.roll(high, (64 - q * 8) % 128, 1),
                    jnp.where(lane >= 120, pltpu.roll(low, (120 - q * 8) % 128, 1), 0.0),
                ),
            )
            if level < 17:
                one[level] = full
            elif level < 32:
                two[level - 16] = full
            else:
                coef[level - 31] = full
    first = lanes((8, 128)) < 64
    now, old = one, two
    for step in range(1, STEPS + 1):
        for j in range(step, 17 - step):
            u = now[j]
            beside = pltpu.roll(u, 1, 0) + pltpu.roll(u, 31, 0) + pltpu.roll(u, 1, 1) + pltpu.roll(u, 127, 1)
            lap = beside + now[j - 1] + now[j + 1] - 6.0 * u
            old[j] = 2.0 * u - old[j] + coef[j] * lap
        now, old = old, now
        plane = now[8]
        trace[:, step - 1, :] = jnp.where(first, plane[0:8], pltpu.roll(plane[8:16], 64, 1))
    for peer in range(copies.shape[0]):
        copies[peer] = trace[...]


def pick_kernel(table, index, *outs):
    me = lax.axis_index("gy")
    count = table.shape[0]

    def tile(row):
        cell = jnp.broadcast_to(index[pl.ds(row, 1), :], (8, 128))
        x, y = cell >> 8, cell & 255
        place = ((x >> 4) << 3) + (x & 7)
        place = jnp.where((y >> 6) == me, place, -1)
        lane = (((x >> 3) & 1) << 6) + (y & 63)
        accs = [jnp.zeros((8, 128), F32) for _ in range(4)]
        for k in range(count):
            found = jnp.take_along_axis(table[k], lane, axis=1)
            accs[k % 4] = jnp.where(place == k, found, accs[k % 4])
        return (accs[0] + accs[1]) + (accs[2] + accs[3])

    def tiles(t, carry):
        for j, out in enumerate(outs):
            out[t] = tile(lax.rem(me + j, 4) * 4 + t)
        return carry

    lax.fori_loop(0, 4, tiles, 0)


def spring_values(cls, k, count, modulus, yields):
    mod = jnp.zeros(cls.shape, F32)
    lim = jnp.zeros(cls.shape, F32)
    for c in range(8):
        hit = cls == c
        mod = jnp.where(hit, modulus[c, k], mod)
        lim = jnp.where(hit, jnp.where(k < count[c], yields[c, k], 0.0), lim)
    return mod, lim


def columns_kernel(count, modulus, yields, soil, start, out, edge, mods, lims, springs):
    width = soil.shape[1]

    def rows(r, carry):
        at = pl.ds(pl.multiple_of(r * 8, 8), 8)
        cls = soil[at, :]
        for k in range(16):
            mod, lim = spring_values(cls, k, count, modulus, yields)
            mods[k, at, :] = mod
            lims[k, at, :] = lim
            springs[k, at, :] = jnp.zeros((8, width), F32)
        return carry

    lax.fori_loop(0, 8, rows, 0)
    row = lax.broadcasted_iota(jnp.int32, (64, width), 0)

    def step(s, state):
        disp, vel, old = state
        strain = pltpu.roll(disp, 63, 0) - disp
        inc = strain - old
        parts = []
        for r in range(0, 64, 16):
            here = slice(r, r + 16)
            change = inc[here]
            stress = jnp.zeros((16, width), F32)
            for k in range(16):
                lim = lims[k, here, :]
                value = jnp.minimum(jnp.maximum(springs[k, here, :] + mods[k, here, :] * change, -lim), lim)
                springs[k, here, :] = value
                stress = stress + value
            parts.append(stress)
        stress = jnp.concatenate(parts, axis=0)
        edge[pl.ds(s, 1), :] = stress[55:56]
        above = jnp.where(row == 0, 0.0, pltpu.roll(stress, 1, 0))
        vel = vel + stress_rate * (stress - above)
        return disp + vel, vel, strain

    zero = jnp.zeros((64, width), F32)
    out[...] = lax.fori_loop(0, STEPS, step, (start[...], zero, zero))[0]


def last_rows_kernel(count, modulus, yields, soil, start, edge, own, next1, next2, next3, done, out):
    del done
    row = lax.broadcasted_iota(jnp.int32, (8, 128), 0)
    for t in range(4):
        cols = slice(t * 128, (t + 1) * 128)
        base = (own[t] + next1[t]) + (next2[t] + next3[t])
        cls = soil[:, cols]
        pairs = [spring_values(cls, k, count, modulus, yields) for k in range(16)]
        springs = [jnp.zeros((8, 128), F32) for _ in range(16)]
        disp = start[:, cols]
        vel = jnp.zeros((8, 128), F32)
        old = jnp.zeros((8, 128), F32)
        for s in range(STEPS):
            strain = jnp.where(row == 7, base[s : s + 1], pltpu.roll(disp, 7, 0)) - disp
            inc = strain - old
            old = strain
            for k in range(16):
                mod, lim = pairs[k]
                springs[k] = jnp.minimum(jnp.maximum(springs[k] + mod * inc, -lim), lim)
            sums = springs
            while len(sums) > 1:
                sums = [sums[i] + sums[i + 1] for i in range(0, len(sums), 2)]
            stress = sums[0]
            above = jnp.where(row == 0, edge[s : s + 1, cols], pltpu.roll(stress, 1, 0))
            vel = vel + stress_rate * (stress - above)
            disp = disp + vel
        out[:, cols] = disp


RIGHT = ((8, 8, 0), (9, 7, 8), (9, 7, 15))
LEFT = ((0, 8, 0), (0, 7, 8), (0, 7, 15))


def start_jobs(jobs, sems):
    copies = [(cond, pltpu.make_async_copy(src, dst, sems.at[n])) for n, (cond, src, dst) in enumerate(jobs)]
    for cond, copy in copies:
        if cond is None:
            copy.start()
        else:
            pl.when(cond)(copy.start)
    return copies


def wait_jobs(copies):
    for cond, copy in copies:
        if cond is None:
            copy.wait()
        else:
            pl.when(cond)(copy.wait)


def run_jobs(jobs, sems):
    wait_jobs(start_jobs(jobs, sems))


def pack_x_kernel(u, p, c, edge_right, edge_left, mid_right, mid_left, mid_far, sems):
    jobs = []
    gx = lax.axis_index("gx")
    for plan, edge, mid, ends in (
        (RIGHT, edge_right, mid_right, gx == lax.axis_size("gx") - 1),
        (LEFT, edge_left, mid_left, gx == 0),
    ):
        for ref, (x0, n, at) in zip((u, p, c), plan):
            middle = ref.at[x0 : x0 + n, 8:56, :]
            jobs.append((None, ref.at[x0 : x0 + n, 0:8, :], edge.at[at : at + n, 0:8, :]))
            jobs.append((None, ref.at[x0 : x0 + n, 56:64, :], edge.at[at : at + n, 8:16, :]))
            jobs.append((None, middle, mid.at[at : at + n, :, :]))
            jobs.append((ends, middle, mid_far.at[at : at + n, :, :]))
    run_jobs(jobs, sems)


def pack_y_kernel(u, p, c, from_left, from_right, send_a, send_b, sems):
    odd = lax.rem(lax.axis_index("gy"), 2)
    pairs = []
    for send, side in ((send_a, 1 - odd), (send_b, odd)):
        own = pl.ds(pl.multiple_of(side * 56, 8), 8)
        corner = pl.ds(pl.multiple_of(side * 8, 8), 8)
        for n, ref in enumerate((u, p, c)):
            pairs.append((None, ref.at[:, own, :], send.at[16 * n : 16 * n + 16]))
        pairs.append((None, from_left.at[:, corner, :], send.at[48:70]))
        pairs.append((None, from_right.at[:, corner, :], send.at[70:92]))
    run_jobs(pairs, sems)


def region_kernel(u, p, c, el, er, ml, mr, relayed, ya, yb, out, one, two, coef, sems):
    low_x, high_x = x_edges()
    low_y, high_y = y_edges()
    even = lax.rem(lax.axis_index("gy"), 2) == 0
    bufs = (one, two, coef)
    gx = lax.axis_index("gx")
    first, final = gx == 0, gx == lax.axis_size("gx") - 1
    jobs = []

    def job(cond, src, dst):
        jobs.append((cond, src, dst))

    for ref, buf in zip((u, p, c), bufs):
        job(None, ref, buf.at[0:16, 16:80, :])
    left_at = ((24, 8, 0), (25, 7, 8), (25, 7, 15))
    right_at = ((16, 8, 0), (16, 7, 8), (16, 7, 15))
    for cond, far, plan, edge, mid in ((~low_x, first, left_at, el, ml), (~high_x, final, right_at, er, mr)):
        for buf, (x0, n, at) in zip(bufs, plan):
            job(~far, mid.at[at : at + n], buf.at[x0 : x0 + n, 24:72, :])
            job(far & cond, relayed.at[at : at + n], buf.at[x0 : x0 + n, 24:72, :])
            job(cond, edge.at[at : at + n, 0:8, :], buf.at[x0 : x0 + n, 16:24, :])
            job(cond, edge.at[at : at + n, 8:16, :], buf.at[x0 : x0 + n, 72:80, :])
    for msg, is_high in ((ya, even), (yb, ~even)):
        for rows, cond in (((80, 88), is_high & ~high_y), ((8, 16), ~is_high & ~low_y)):
            for n, buf in enumerate(bufs):
                job(cond, msg.at[16 * n : 16 * n + 16], buf.at[0:16, rows[0] : rows[1], :])
            for more, plan, base in ((~low_x, left_at, 48), (~high_x, right_at, 70)):
                for buf, (x0, n, at) in zip(bufs, plan):
                    job(
                        cond & more,
                        msg.at[base + at : base + at + n],
                        buf.at[x0 : x0 + n, rows[0] : rows[1], :],
                    )
    copies = start_jobs(jobs, sems)
    for edge, x0, n, y0, m in (
        (low_x, 24, 8, 8, 80),
        (high_x, 16, 8, 8, 80),
        (low_y, 0, 32, 8, 8),
        (high_y, 0, 32, 80, 8),
    ):

        @pl.when(edge)
        def _():
            for buf in bufs:
                buf[x0 : x0 + n, y0 : y0 + m, :] = jnp.zeros((n, m, 256), F32)

    wait_jobs(copies)

    now, old = one, two
    halves = (slice(0, 128), slice(128, 256))
    rows = 16
    lane = lanes((rows, 128))
    top, end = lane == 0, lane == 127
    for step in range(1, STEPS + 1):
        last = step == STEPS
        for x in range(step - HALO, 16 + HALO - step):
            at, lower, upper = x % 32, (x - 1) % 32, (x + 1) % 32
            for y0 in range(16, 80, rows) if last else range(8, 88, rows):
                here = slice(y0, y0 + rows)
                a, b = (now[at, here, h] for h in halves)
                ra, rb = pltpu.roll(a, 1, 1), pltpu.roll(b, 1, 1)
                la, lb = pltpu.roll(a, 127, 1), pltpu.roll(b, 127, 1)
                depth = (
                    jnp.where(top, a, ra) + jnp.where(end, lb, la),
                    jnp.where(top, ra, rb) + jnp.where(end, 0.0, lb),
                )
                for h, v, dz in zip(halves, (a, b), depth):
                    beside = now[lower, here, h] + now[upper, here, h]
                    beside = beside + (now[at, y0 - 1 : y0 - 1 + rows, h] + now[at, y0 + 1 : y0 + 1 + rows, h])
                    lap = beside + dz - 6.0 * v
                    value = (2.0 * v - old[at, here, h]) + coef[at, here, h] * lap
                    if last:
                        out[x, y0 - 16 : y0 - 16 + rows, h] = value
                    else:
                        old[at, here, h] = value
        now, old = old, now


def relays(n_sec, n_gx):
    def at(sec, gx, gy):
        return (sec % n_sec * n_gx + gx) * 4 + gy

    top = n_gx - 1
    out, into = [], []
    for sec in range(n_sec):
        for gy in range(4):
            up, down = ((3, 12), (11, 4))[gy % 2]
            out += [(at(sec, top, gy), at(sec, up, gy)), (at(sec, 0, gy), at(sec, down, gy))]
            if sec < n_sec - 1:
                into.append((at(sec, up, gy), at(sec + 1, 0, gy)))
            if sec > 0:
                into.append((at(sec, down, gy), at(sec - 1, top, gy)))
    return out, into


def shards(
    reg_disp,
    reg_prev,
    reg_coef,
    basin_disp,
    face_index,
    soil_class,
    spring_count,
    spring_modulus,
    spring_yield,
):
    n_gx = lax.axis_size("gx")
    n_x = lax.axis_size("sec") * n_gx
    right = [(i, (i + 1) % n_x) for i in range(n_x)]
    left = [(i, (i - 1) % n_x) for i in range(n_x)]
    swap_a = [(0, 1), (1, 0), (2, 3), (3, 2)]
    swap_b = [(0, 0), (1, 2), (2, 1), (3, 3)]
    regional = (reg_disp, reg_prev, reg_coef)
    half = pl.BlockSpec((16, 64, 128), lambda i: (0, 0, 0))
    whole = lambda *s: pl.BlockSpec(s, lambda i: (0,) * len(s))
    band, band_right, band_left = pl.pallas_call(
        band_kernel,
        grid=(1,),
        out_shape=(sds(48, 8, 128), sds(24, 8, 128), sds(24, 8, 128)),
        in_specs=[half] * 3,
        out_specs=(whole(48, 8, 128), whole(24, 8, 128), whole(24, 8, 128)),
        compiler_params=LARGE,
        name="band",
    )(*regional)
    band_from_left = lax.ppermute(band_right, XAX, right)
    band_from_right = lax.ppermute(band_left, XAX, left)
    index, _ = lax.optimization_barrier((face_index.reshape(1, 4, 128), band_right))
    index = lax.all_gather(index, "gy").reshape(16, 128)

    regional, index = lax.optimization_barrier((regional, index))
    edge_right, edge_left, mid_right, mid_left, mid_far = pl.pallas_call(
        pack_x_kernel,
        out_shape=(sds(22, 16, 256), sds(22, 16, 256), sds(22, 48, 256), sds(22, 48, 256), sds(22, 48, 256)),
        in_specs=[ANY] * 3,
        out_specs=(ANY,) * 5,
        scratch_shapes=[pltpu.SemaphoreType.DMA((24,))],
        compiler_params=PARAMS,
        name="pack_x",
    )(*regional)
    edge_from_left = lax.ppermute(edge_right, XAX, right)
    edge_from_right = lax.ppermute(edge_left, XAX, left)

    soil = soil_class[0]
    start = basin_disp[0]
    soil, start, _ = lax.optimization_barrier((soil, start, index))
    tables = (spring_count, spring_modulus, spring_yield)
    block = pl.BlockSpec((64, 256), lambda i: (0, i))
    upper, edge = pl.pallas_call(
        columns_kernel,
        grid=(2,),
        out_shape=(sds(64, 512), sds(8, 512)),
        in_specs=[SM] * 3 + [block] * 2,
        out_specs=(block, pl.BlockSpec((8, 256), lambda i: (0, i))),
        scratch_shapes=[pltpu.VMEM((16, 64, 256), F32)] * 3,
        compiler_params=PARAMS,
        name="columns",
    )(*tables, soil, start)

    upper, band_from_left, band_from_right = lax.optimization_barrier((upper, band_from_left, band_from_right))
    relay_out, relay_in = relays(lax.axis_size("sec"), n_gx)
    mid_far, band_from_left, band_from_right = lax.optimization_barrier((mid_far, band_from_left, band_from_right))
    mid_relay = lax.ppermute(mid_far, ALL, relay_out)
    mid_relay = lax.ppermute(mid_relay, ALL, relay_in)

    ext, band_a, band_b = pl.pallas_call(
        band_edges_kernel,
        out_shape=(sds(48, 32, 128), sds(3, 32, 128), sds(3, 32, 128)),
        in_specs=[VM] * 3,
        out_specs=(VM,) * 3,
        compiler_params=PARAMS,
        name="band_edges",
    )(band, band_from_left, band_from_right)
    band_a = lax.ppermute(band_a, "gy", swap_a)
    band_b = lax.ppermute(band_b, "gy", swap_b)
    trace = pl.pallas_call(
        band_steps_kernel,
        out_shape=sds(n_gx, 8, 8, 128),
        in_specs=[VM] * 3,
        out_specs=VM,
        scratch_shapes=[pltpu.VMEM((17, 32, 128), F32)] * 3 + [pltpu.VMEM((8, 8, 128), F32)],
        compiler_params=PARAMS,
        name="band_steps",
    )(ext, band_a, band_b)

    table = lax.all_to_all(trace.reshape(n_gx, 64, 128), "gx", 0, 0)
    table = table.reshape(n_gx * 8, 8, 128)
    mid_from_left = lax.ppermute(mid_right, "gx", [(i, i + 1) for i in range(n_gx - 1)])
    mid_from_right = lax.ppermute(mid_left, "gx", [(i + 1, i) for i in range(n_gx - 1)])
    trace, edge_from_left, edge_from_right = lax.optimization_barrier((trace, edge_from_left, edge_from_right))
    y_a, y_b = pl.pallas_call(
        pack_y_kernel,
        out_shape=(sds(92, 8, 256), sds(92, 8, 256)),
        in_specs=[ANY] * 5,
        out_specs=(ANY,) * 2,
        scratch_shapes=[pltpu.SemaphoreType.DMA((10,))],
        compiler_params=PARAMS,
        name="pack_y",
    )(*regional, edge_from_left, edge_from_right)
    y_a = lax.ppermute(y_a, "gy", swap_a)
    y_b = lax.ppermute(y_b, "gy", swap_b)

    picked = pl.pallas_call(
        pick_kernel,
        out_shape=(sds(4, 8, 128),) * 4,
        in_specs=[VM] * 2,
        out_specs=(VM,) * 4,
        compiler_params=PARAMS,
        name="pick",
    )(table, index)
    y_b, *picked = lax.optimization_barrier((y_b, *picked))
    arrived = [picked[0]] + [
        lax.ppermute(picked[k], "gy", [(i, (i + k) % 4) for i in range(4)]) for k in (1, 2, 3)
    ]

    final = pl.pallas_call(
        region_kernel,
        out_shape=sds(16, 64, 256),
        in_specs=[ANY] * 10,
        out_specs=VM,
        scratch_shapes=[pltpu.VMEM((32, 96, 256), F32)] * 3 + [pltpu.SemaphoreType.DMA((64,))],
        compiler_params=PARAMS,
        name="region",
    )(*regional, edge_from_left, edge_from_right, mid_from_left, mid_from_right, mid_relay, y_a, y_b)
    final, *arrived = lax.optimization_barrier((final, *arrived))
    tail = pl.BlockSpec((8, 512), lambda i: (7, 0))
    basin = pl.pallas_call(
        last_rows_kernel,
        grid=(1,),
        out_shape=sds(64, 512),
        in_specs=[SM] * 3 + [tail, tail, whole(8, 512)] + [whole(4, 8, 128)] * 4 + [ANY],
        out_specs=tail,
        input_output_aliases={10: 0},
        compiler_params=PARAMS,
        name="last_rows",
    )(*tables, soil, start, edge, *arrived, upper)
    return (final, basin[None])


def solution(mesh):
    in_specs = (
        P(("sec", "gx"), "gy", None),
        P(("sec", "gx"), "gy", None),
        P(("sec", "gx"), "gy", None),
        P("sec", None, ("gx", "gy")),
        P("sec", ("gx", "gy")),
        P("sec", None, ("gx", "gy")),
        P(),
        P(),
        P(),
    )
    out_specs = (P(("sec", "gx"), "gy", None), P("sec", None, ("gx", "gy")))
    return jax.shard_map(shards, mesh=mesh, in_specs=in_specs, out_specs=out_specs, check_vma=False)
```
